256 devices in a mesh: dp: 4 (over y), table: 64 (over z, x, core).
Axes of the slice: x: 4, y: 4, z: 8, core: 2. Of those that a mesh axis runs over, the one named last changes fastest.
Arguments:
- table_rows: float32 [24576, 1280], P('table'), may hold values from -1.2 to 1.2
- first_moment: float32 [24576, 1280], P('table'), may hold values from -2 to 2
- second_moment: float32 [24576, 1280], P('table'), may hold values from 0.05 to 5
- grad_rows: bfloat16 [262144, 1280], P(('dp', 'table')), may hold values from -6 to 6
- row_ids: int32 [262144], P(('dp', 'table')), may hold values from 0 to 384, as said below
- next_ids: int32 [262144], P(('dp', 'table')), may hold values from 0 to 384, as said below
Outputs:
- new_table: float32 [24576, 1280], P('table')
- new_first: float32 [24576, 1280], P('table')
- new_second: float32 [24576, 1280], P('table')
- fetched: bfloat16 [262144, 1280], P(('dp', 'table'))
The draws below stay inside these ranges and needn't reach their ends.
Inputs may be any that keep to these rules, and one draw needn't show every extreme that they name: `row_ids`: each block of 16 slots from one device to one owner holds its live rows first and then empty slots marked 384; every draw has blocks with all 16 slots live; rows may repeat. `next_ids`: same layout as row_ids.
All inputs are finite; a program needn't handle non-finite values.
Results may differ from the reference program's by a relative error of at most 0.001.
Values may be sent and summed in bfloat16 or wider, within the bound.
No kernel may reach another device: no remote copies, remote signals or barrier semaphores. Data moves between devices by JAX's collectives and lax.ppermute only.
A program may use at most 64 MiB of HBM per device.

```python
import math
import jax
import jax.numpy as jnp
from jax import lax

E = 1280
ROWS_DEV = 384
STEP = 20
SLOTS = 1024
CAP = 16
ROWS = 24576
SENDERS = 256
N_DP = 4
N_TABLE = 64


def route_ids(key):
    senders = N_DP * N_TABLE
    key_count, key_first, key_second, key_offset = jax.random.split(key, 4)
    count = jax.random.randint(key_count, (senders, N_TABLE, 1), 1, CAP + 1)
    sender = jnp.arange(senders, dtype=jnp.int32)[:, None, None]
    owner = jnp.arange(N_TABLE, dtype=jnp.int32)[None, :, None]
    count = jnp.where((sender + owner) % 4 == 0, CAP, count)
    first = jax.random.randint(key_first, (senders, N_TABLE, CAP), 0, ROWS_DEV)
    second = jax.random.randint(key_second, (senders, N_TABLE, CAP), 0, ROWS_DEV)
    offset = jax.random.randint(key_offset, (1, N_TABLE, 1), 0, ROWS_DEV)
    row = (jnp.minimum(first, second) + offset) % ROWS_DEV
    position = jnp.arange(CAP, dtype=jnp.int32)[None, None, :]
    ids = jnp.where(position < count, row, ROWS_DEV)
    return ids.reshape(senders * N_TABLE * CAP).astype(jnp.int32)


def draw_row_ids(key, part):
    key = jax.random.fold_in(key, 11)
    return route_ids(key)


def draw_next_ids(key, part):
    key = jax.random.fold_in(key, 23)
    return route_ids(key)


def level_of(own_key, extent, pieces, smallest, high):
    def one(dim, blocks):
        steps = jax.random.uniform(jax.random.fold_in(jax.random.fold_in(own_key, 6), dim), (blocks,), jnp.float32, smallest / len(pieces), high / len(pieces))
        return jnp.repeat(jnp.exp(steps), extent[dim] // blocks).reshape((-1,) + (1,) * (len(extent) - dim - 1))

    level = one(*pieces[0])
    for cut in pieces[1:]:
        level = level * one(*cut)
    return level


def gaussian(rng, dims, scale, limit, cuts=(), kind=jnp.bfloat16):
    loudness = level_of(rng, dims, cuts, -0.22, 0.18) if cuts else 1.0
    drawn = jax.random.normal(rng, dims, jnp.float32) * scale * loudness
    return jnp.minimum(jnp.maximum(drawn, -limit), limit).astype(kind)


def setup_inputs(seed: int = 0) -> dict:
    splits = jax.random.split(jax.random.key(seed), 7)
    return {
        "table_rows": gaussian(splits[0], (ROWS, E), 0.3, 1.2, ((0, 64),), jnp.float32),
        "first_moment": gaussian(splits[1], (ROWS, E), 0.3, 2.0, ((0, 64),), jnp.float32),
        "second_moment": jnp.clip(jnp.exp(math.log(5.0) - 4.6051702 * jax.random.uniform(splits[2], (ROWS, E), jnp.float32) ** level_of(splits[2], (ROWS, E), ((0, 64),), -0.2, 0.2)), 0.05, 5.0),
        "grad_rows": gaussian(splits[3], (SENDERS * SLOTS, E), 1.0, 6.0, ((0, 256),)),
        "row_ids": draw_row_ids(jax.random.fold_in(splits[6], 71), 0),
        "next_ids": draw_next_ids(jax.random.fold_in(splits[6], 71), 0),
    }


def adamw(weights, first, second, grads):
    first_new = 0.9 * first + 0.1 * grads
    second_new = 0.95 * second + 0.05 * grads * grads
    corr_one = 1.0 - 0.9 ** STEP
    corr_two = 1.0 - 0.95 ** STEP
    update = first_new / corr_one / (jnp.sqrt(second_new / corr_two) + 1e-08) + 0.01 * weights
    return (weights - 0.1 * update, first_new, second_new)

def global_rows(ids, total_rows):
    owner = jnp.arange(ids.shape[0], dtype=jnp.int32) % SLOTS // CAP
    return jnp.where(ids < ROWS_DEV, owner * ROWS_DEV + ids, total_rows).astype(jnp.int32)

def reference(table_rows, first_moment, second_moment, grad_rows, row_ids, next_ids):
    total_rows = table_rows.shape[0]
    width = table_rows.shape[1]
    targets = global_rows(row_ids, total_rows).reshape(SENDERS, SLOTS)
    grads = grad_rows.reshape(SENDERS, SLOTS, width)

    def accumulate(total, item):
        block, where = item
        return (total.at[where].add(block.astype(jnp.float32)), None)
    summed, unused = lax.scan(accumulate, jnp.zeros((total_rows + 1, width), jnp.float32), (grads, targets))
    new_table, new_first, new_second = adamw(table_rows, first_moment, second_moment, summed[:total_rows])
    padded = jnp.concatenate([new_table.astype(jnp.bfloat16), jnp.zeros((1, width), jnp.bfloat16)], 0)
    fetched = jnp.take(padded, global_rows(next_ids, total_rows), axis=0)
    return (new_table, new_first, new_second, fetched)
```

```python
import jax
import jax.numpy as jnp
from jax import lax
from jax.experimental import pallas as pl
from jax.experimental.pallas import tpu as pltpu
from jax.sharding import Mesh, PartitionSpec as P

STEP = 20
LANES = 128
CAP = 16
BF = jnp.bfloat16
F32 = jnp.float32
F16 = jnp.float16
SLAB = ("y", "x", "c")
GROUP = 32
NZ = 8
NY = 4
XC = 8
ROWS = 384
HALF = 192
QROWS = 960
SENT = 336
BACK = 320


def adamw(weights, first, second, grads):
    first_new = 0.9 * first + 0.1 * grads
    second_new = 0.95 * second + 0.05 * grads * grads
    corr_one = 1.0 - 0.9**STEP
    corr_two = 1.0 - 0.95**STEP
    update = first_new / corr_one / (jnp.sqrt(second_new / corr_two) + 1e-08) + 0.01 * weights
    return (weights - 0.1 * update, first_new, second_new)


def low_lanes(shape):
    return lax.broadcasted_iota(jnp.int32, shape, len(shape) - 1) < 64


def pair(a, b, upper):
    low = low_lanes(a.shape)
    axis = a.ndim - 1
    if isinstance(upper, bool):
        return jnp.where(low, pltpu.roll(a, 64, axis), b) if upper else jnp.where(low, a, pltpu.roll(b, 64, axis))
    return jnp.where(
        upper,
        jnp.where(low, pltpu.roll(a, 64, axis), b),
        jnp.where(low, a, pltpu.roll(b, 64, axis)),
    )


def params(mib):
    return pltpu.CompilerParams(vmem_limit_bytes=mib * 1024 * 1024)


def hbm(x):
    return pltpu.with_memory_space_constraint(x, pltpu.HBM)


def tile_iota(axis):
    return lax.broadcasted_iota(jnp.int32, (8, LANES), axis)


def diagonal(rolled, shift):
    moved = pltpu.roll(rolled, (NZ * LANES - CAP * shift) % LANES, 1)
    kept = jnp.where(tile_iota(1) // CAP == tile_iota(0), moved, 0.0)
    return jnp.sum(kept, axis=0, keepdims=True)


def row_roll(x):
    return pltpu.roll(x, 0, 1, stride=CAP, stride_axis=0)


PACK_STEP = 2


def pack_kernel(g_ref, row_ref, next_ref, o_ref):
    ids = [row_roll(r[...].astype(F32)) for r in (row_ref, next_ref)]
    sub = lax.broadcasted_iota(jnp.int32, (CAP, LANES), 0)
    for u in range(PACK_STEP):
        for y in range(NY):
            for z in range(NZ):
                o_ref[y, u, pl.ds(z * CAP, CAP), :] = g_ref[z, u, :, pl.ds(y * LANES, LANES)]
                o_ref[y, u, pl.ds(128 + z * CAP, CAP), :] = g_ref[z, u, :, pl.ds(512 + y * LANES, LANES)]
            for k in range(NZ // 2):
                cols = pl.ds(1024 + (y // 2) * LANES, LANES)
                a = g_ref[2 * k, u, :, cols].astype(F32)
                b = g_ref[2 * k + 1, u, :, cols].astype(F32)
                o_ref[y, u, pl.ds(256 + k * CAP, CAP), :] = pair(a, b, y % 2 == 1).astype(BF)
        head = jnp.zeros((CAP, LANES), F32)
        for t in range(2):
            mine = diagonal(ids[t], pl.program_id(0) * PACK_STEP + u)
            upper = jnp.floor(mine * (1.0 / 16.0))
            head = jnp.where(sub == 2 * t, upper, head)
            head = jnp.where(sub == 2 * t + 1, mine - 16.0 * upper, head)
        for y in range(NY):
            o_ref[y, u, pl.ds(BACK, CAP), :] = head.astype(BF)


def pack(grad_rows, row_ids, next_ids):
    whole = pl.BlockSpec((8, LANES), lambda i: (0, 0))
    return pl.pallas_call(
        pack_kernel,
        grid=(XC // PACK_STEP,),
        in_specs=[pl.BlockSpec((NZ, PACK_STEP, CAP, 1280), lambda i: (0, i, 0, 0)), whole, whole],
        out_specs=pl.BlockSpec((NY, PACK_STEP, SENT, LANES), lambda i: (0, i, 0, 0)),
        out_shape=pltpu.HBM((NY, XC, SENT, LANES), BF),
        compiler_params=params(12),
        name="pack",
    )(
        hbm(grad_rows.reshape(NZ, XC, CAP, 1280)),
        hbm(row_ids.reshape(8, LANES)),
        hbm(next_ids.reshape(8, LANES)),
    )


def reduce_kernel(z_ref, got_ref, o_ref, next_ref, ids_ref):
    sub = tile_iota(0)
    for q in range(GROUP // 8):
        tiles = [jnp.zeros((8, LANES), F32)] * 2
        for j in range(8):
            head = got_ref[8 * q + j, pl.ds(BACK, CAP), :].astype(F32)
            for t in range(2):
                mine = head[2 * t : 2 * t + 1] * 16.0 + head[2 * t + 1 : 2 * t + 2]
                tiles[t] = jnp.where(sub == j, mine, tiles[t])
        for t, ref in ((0, ids_ref), (1, next_ref)):
            rolled = row_roll(tiles[t])
            for k in range(NZ):
                ref[pl.ds(k, 1), pl.ds(q * LANES, LANES)] = diagonal(rolled, z_ref[0] + k).astype(jnp.int32)
    rows = lax.broadcasted_iota(jnp.int32, (ROWS, GROUP * CAP), 0)
    for k in range(NZ):
        z = (z_ref[0] + k) % NZ
        pick = jnp.where(rows == ids_ref[pl.ds(k, 1), :], 1.0, 0.0).astype(BF)
        starts = (z * CAP, 128 + z * CAP, 256 + (z // 2) * CAP)
        slots = jnp.concatenate(
            [got_ref[:, pl.ds(pl.multiple_of(at, CAP), CAP), :].reshape(GROUP * CAP, LANES) for at in starts], axis=1
        )
        total = jnp.dot(pick, slots, preferred_element_type=F32)
        o_ref[k, pl.ds(0, ROWS), :] = total[:, :128]
        o_ref[k, pl.ds(ROWS, ROWS), :] = total[:, 128:256]
        last = total[:, 256:]
        o_ref[k, pl.ds(2 * ROWS, HALF), :] = pair(last[:HALF], last[HALF:], z % 2 == 1)


def partial_sums(z, got):
    vmem = pl.BlockSpec(memory_space=pltpu.VMEM)
    smem = pl.BlockSpec(memory_space=pltpu.SMEM)
    return pl.pallas_call(
        reduce_kernel,
        in_specs=[smem, vmem],
        out_specs=[vmem, vmem],
        out_shape=[
            jax.ShapeDtypeStruct((NZ, QROWS, LANES), F32),
            jax.ShapeDtypeStruct((NZ, GROUP * CAP), jnp.int32),
        ],
        scratch_shapes=[pltpu.VMEM((NZ, GROUP * CAP), jnp.int32)],
        compiler_params=params(16),
        name="partial_sums",
    )(z, got)


def quarter_kernel(y_ref, *refs):
    odd = y_ref[0] % 2 == 1
    for i in range(3):
        a, b, c = (r[...] for r in refs[3 * i : 3 * i + 3])
        o_ref = refs[9 + i]
        o_ref[pl.ds(0, ROWS), :] = a
        o_ref[pl.ds(ROWS, ROWS), :] = b
        o_ref[pl.ds(2 * ROWS, HALF), :] = pair(c[:HALF], c[HALF:], odd)


def quarters(y, *arrays):
    spec = [
        pl.BlockSpec((ROWS, LANES), lambda i, s: (0, s[0])),
        pl.BlockSpec((ROWS, LANES), lambda i, s: (0, NY + s[0])),
        pl.BlockSpec((ROWS, LANES), lambda i, s: (0, 2 * NY + s[0] // 2)),
    ]
    return pl.pallas_call(
        quarter_kernel,
        grid_spec=pltpu.PrefetchScalarGridSpec(
            num_scalar_prefetch=1,
            grid=(1,),
            in_specs=spec * 3,
            out_specs=[pl.BlockSpec((QROWS, LANES), lambda i, s: (0, 0))] * 3,
        ),
        out_shape=[jax.ShapeDtypeStruct((QROWS, LANES), F32)] * 3,
        compiler_params=params(12),
        cost_estimate=pl.CostEstimate(flops=1_000_000, bytes_accessed=3_000_000, transcendentals=0),
        name="quarters",
    )(y, *[hbm(t) for t in arrays for _ in range(3)])


def fetch_kernel(z_ref, ids_ref, *refs):
    tables, o_ref = refs[:NZ], refs[NZ]
    low = low_lanes((GROUP, CAP, LANES))
    rows = lax.broadcasted_iota(jnp.int32, (GROUP * CAP, ROWS), 1).astype(F32)
    columns = jnp.transpose(ids_ref[...].astype(F32))
    for k in range(NZ):
        z = (z_ref[0] + k) % NZ
        pick = jnp.where(rows == columns[:, k : k + 1], 1.0, 0.0).astype(BF)
        table = tables[k]
        last = table[pl.ds(2 * ROWS, HALF), :].astype(F32)
        moved = pltpu.roll(last, 64, 1)
        odd = z % 2 == 1
        lower = jnp.where(odd, moved, last).astype(BF)
        higher = jnp.where(odd, last, moved).astype(BF)
        wide = jnp.concatenate(
            [table[pl.ds(0, ROWS), :], table[pl.ds(ROWS, ROWS), :], jnp.concatenate([lower, higher], axis=0)],
            axis=1,
        )
        found = jnp.dot(pick, wide, preferred_element_type=F32)
        found = found.astype(BF).reshape(GROUP, CAP, 3 * LANES)
        at = pl.multiple_of(z * CAP, CAP)
        o_ref[:, pl.ds(at, CAP), :] = found[:, :, :128]
        o_ref[:, pl.ds(at + 128, CAP), :] = found[:, :, 128:256]
        both = pl.ds(pl.multiple_of(256 + (z // 2) * CAP, CAP), CAP)
        old = o_ref[:, both, :]
        o_ref[:, both, :] = jnp.where(low == odd, old, found[:, :, 256:])


def fetch(z, ids, tables):
    vmem = pl.BlockSpec(memory_space=pltpu.VMEM)
    return pl.pallas_call(
        fetch_kernel,
        in_specs=[pl.BlockSpec(memory_space=pltpu.SMEM)] + [vmem] * 9,
        out_specs=vmem,
        out_shape=jax.ShapeDtypeStruct((GROUP, BACK, LANES), BF),
        compiler_params=params(16),
        name="fetch",
    )(z, ids, *tables)


UNPACK_STEP = 2


def unpack_kernel(g_ref, o_ref):
    for u in range(UNPACK_STEP):
        for y in range(NY):
            for z in range(NZ):
                o_ref[z, u, :, pl.ds(y * LANES, LANES)] = g_ref[y, u, pl.ds(z * CAP, CAP), :]
                o_ref[z, u, :, pl.ds(512 + y * LANES, LANES)] = g_ref[y, u, pl.ds(128 + z * CAP, CAP), :]
        for t in range(2):
            for k in range(NZ // 2):
                a = g_ref[2 * t, u, pl.ds(256 + k * CAP, CAP), :].astype(F32)
                b = g_ref[2 * t + 1, u, pl.ds(256 + k * CAP, CAP), :].astype(F32)
                cols = pl.ds(1024 + t * LANES, LANES)
                o_ref[2 * k, u, :, cols] = pair(a, b, False).astype(BF)
                o_ref[2 * k + 1, u, :, cols] = pair(a, b, True).astype(BF)


def unpack(back):
    out = pl.pallas_call(
        unpack_kernel,
        grid=(XC // UNPACK_STEP,),
        in_specs=[pl.BlockSpec((NY, UNPACK_STEP, BACK, LANES), lambda i: (0, i, 0, 0))],
        out_specs=pl.BlockSpec((NZ, UNPACK_STEP, CAP, 1280), lambda i: (0, i, 0, 0)),
        out_shape=pltpu.HBM((NZ, XC, CAP, 1280), BF),
        compiler_params=params(12),
        name="unpack",
    )(back.reshape(NY, XC, BACK, LANES))
    return out.reshape(NZ * XC * CAP, 1280)


FULL_STEP = 48


def full_kernel(y_ref, *refs):
    g_refs, (w_ref, m_ref, v_ref, ow_ref, om_ref, ov_ref, all_ref) = refs[:NY], refs[NY:]
    for d in range(NY):
        all_ref[(y_ref[0] + d) % NY] = g_refs[d][...]
    for half in range(2):
        for t in range(10):
            if t < 8:
                grads = all_ref[t % NY, 2 * (t // NY) + half]
            else:
                grads = pair(all_ref[2 * (t - 8), 4], all_ref[2 * (t - 8) + 1, 4], half == 1)
            cols = pl.ds(t * LANES, LANES)
            w, m, v = adamw(w_ref[half, :, cols], m_ref[half, :, cols], v_ref[half, :, cols], grads)
            ow_ref[half, :, cols] = w
            om_ref[half, :, cols] = m
            ov_ref[half, :, cols] = v


def full_rows(y, grads, table_rows, first_moment, second_moment):
    wide = pl.BlockSpec((2, FULL_STEP, 1280), lambda i, s: (0, i, 0))
    part = pl.BlockSpec((5, FULL_STEP, LANES), lambda i, s: (0, i, 0))
    outs = pl.pallas_call(
        full_kernel,
        grid_spec=pltpu.PrefetchScalarGridSpec(
            num_scalar_prefetch=1,
            grid=(HALF // FULL_STEP,),
            in_specs=[part] * NY + [wide] * 3,
            out_specs=[wide] * 3,
            scratch_shapes=[pltpu.VMEM((NY, 5, FULL_STEP, LANES), F32)],
        ),
        out_shape=[pltpu.HBM((2, HALF, 1280), F32)] * 3,
        compiler_params=params(12),
        cost_estimate=pl.CostEstimate(flops=10_000_000, bytes_accessed=14_000_000, transcendentals=0),
        name="full_rows",
    )(
        y,
        *[g.reshape(5, HALF, LANES) for g in grads],
        *[hbm(t.reshape(2, HALF, 1280)) for t in (table_rows, first_moment, second_moment)],
    )
    return tuple(t.reshape(ROWS, 1280) for t in outs)


def along(value, axis, size, step):
    return lax.ppermute(value, axis, [(i, (i + step) % size) for i in range(size)])


def send_root(x, step):
    root = jnp.sqrt(jnp.abs(x)) * 256.0
    got = along(jnp.where(x < 0.0, -root, root).astype(F16), "z", NZ, step).astype(F32)
    return got * jnp.abs(got) * (1.0 / 65536.0)


def reduce_z(part):
    up = send_root(part[4], 1)
    down = send_root(part[5], -1)
    for k in (3, 2):
        up = send_root(part[k] + up, 1)
        down = send_root(part[9 - k] + down, -1)
    return part[0] + down + send_root(part[1] + up, 1)


def gather_z(own):
    got = {0: own}
    up = down = own
    for k in (1, 2, 3):
        up, down = along(up, "z", NZ, 1), along(down, "z", NZ, -1)
        got[NZ - k], got[k] = up, down
    got[4] = along(up, "z", NZ, 1)
    return [got[k] for k in range(NZ)]


def gather_y(own):
    return [own] + [along(own, "y", NY, -d) for d in range(1, NY)]


def local(table_rows, first_moment, second_moment, grad_rows, row_ids, next_ids):
    z = lax.axis_index("z").astype(jnp.int32)[None]
    y = lax.axis_index("y").astype(jnp.int32)[None]
    sent = pack(grad_rows, row_ids, next_ids)
    got = lax.all_to_all(sent.reshape(GROUP, SENT, LANES), SLAB, split_axis=0, concat_axis=0, tiled=True)
    mine = quarters(y, table_rows, first_moment, second_moment)
    part, wanted = partial_sums(z, got)
    summed = reduce_z(part)
    own = adamw(*mine, summed)[0].astype(BF)
    tables, grads = lax.optimization_barrier((gather_z(own), gather_y(summed)))
    found = fetch(z, wanted, tables)
    back = lax.all_to_all(found, SLAB, split_axis=0, concat_axis=0, tiled=True)
    outs = full_rows(y, grads, table_rows, first_moment, second_moment)
    return (*outs, unpack(back))


def solution(mesh):
    fine = Mesh(mesh.devices.reshape(NY, NZ, 4, 2), ("y", "z", "x", "c"))
    owner = ("z", "x", "c")
    every = ("y", "z", "x", "c")
    return jax.shard_map(
        local,
        mesh=fine,
        in_specs=(P(owner, None), P(owner, None), P(owner, None), P(every, None), P(every), P(every)),
        out_specs=(P(owner, None), P(owner, None), P(owner, None), P(every, None)),
        check_vma=False,
    )
```

```python
import functools

import jax
import jax.numpy as jnp
from jax import lax
from jax.experimental import pallas as pl
from jax.experimental.pallas import tpu as pltpu
from jax.sharding import Mesh, PartitionSpec as P

STEP = 20
LANES = 128
CAP = 16
BF = jnp.bfloat16
F32 = jnp.float32
F16 = jnp.float16
SLAB = ("y", "x", "c")
GROUP = 32
NZ = 8
NY = 4
XC = 8
ROWS = 384
HALF = 192
QROWS = 960


def adamw(weights, first, second, grads):
    first_new = 0.9 * first + 0.1 * grads
    second_new = 0.95 * second + 0.05 * grads * grads
    corr_one = 1.0 - 0.9**STEP
    corr_two = 1.0 - 0.95**STEP
    update = first_new / corr_one / (jnp.sqrt(second_new / corr_two) + 1e-08) + 0.01 * weights
    return (weights - 0.1 * update, first_new, second_new)


def low_lanes(shape):
    return lax.broadcasted_iota(jnp.int32, shape, len(shape) - 1) < 64


def pair(a, b, upper):
    low = low_lanes(a.shape)
    axis = a.ndim - 1
    if isinstance(upper, bool):
        return jnp.where(low, pltpu.roll(a, 64, axis), b) if upper else jnp.where(low, a, pltpu.roll(b, 64, axis))
    return jnp.where(
        upper,
        jnp.where(low, pltpu.roll(a, 64, axis), b),
        jnp.where(low, a, pltpu.roll(b, 64, axis)),
    )


def params(mib):
    return pltpu.CompilerParams(vmem_limit_bytes=mib * 1024 * 1024)


def hbm(x):
    return pltpu.with_memory_space_constraint(x, pltpu.HBM)


def tile_iota(axis):
    return lax.broadcasted_iota(jnp.int32, (8, LANES), axis)


def diagonal(rolled, shift):
    moved = pltpu.roll(rolled, (NZ * LANES - CAP * shift) % LANES, 1)
    kept = jnp.where(tile_iota(1) // CAP == tile_iota(0), moved, 0.0)
    return jnp.sum(kept, axis=0, keepdims=True)


def row_roll(x):
    return pltpu.roll(x, 0, 1, stride=CAP, stride_axis=0)


def chunk_rows(n):
    return 2 * CAP * n + CAP * ((n + 1) // 2)


def pack_kernel(n, step, with_ids, z_ref, *refs):
    blocks, o_ref = refs[:n], refs[-1]
    sub = lax.broadcasted_iota(jnp.int32, (CAP, LANES), 0)
    if with_ids:
        ids = [row_roll(r[...].astype(F32)) for r in refs[n : n + 2]]
    for u in range(step):
        rest = jnp.zeros((CAP, LANES), F32)
        if with_ids:
            for t in range(2):
                mine = diagonal(ids[t], pl.program_id(0) * step + u)
                upper = jnp.floor(mine * (1.0 / 16.0))
                lower = mine - 16.0 * upper
                for r, row in enumerate((pltpu.roll(upper, 64, 1), upper, pltpu.roll(lower, 64, 1), lower)):
                    rest = jnp.where(sub == 4 * t + r, row, rest)
        for y in range(NY):
            for p in range(n):
                o_ref[y, u, pl.ds(p * CAP, CAP), :] = blocks[p][0, u, :, pl.ds(y * LANES, LANES)]
                o_ref[y, u, pl.ds((n + p) * CAP, CAP), :] = blocks[p][0, u, :, pl.ds(512 + y * LANES, LANES)]
            cols = pl.ds(1024 + (y // 2) * LANES, LANES)
            for t in range((n + 1) // 2):
                a = blocks[2 * t][0, u, :, cols].astype(F32)
                if 2 * t + 1 < n:
                    tile = pair(a, blocks[2 * t + 1][0, u, :, cols].astype(F32), y % 2 == 1)
                else:
                    tile = jnp.where(low_lanes(a.shape), pltpu.roll(a, 64, 1) if y % 2 else a, rest)
                o_ref[y, u, pl.ds((2 * n + t) * CAP, CAP), :] = tile.astype(BF)


def pack(z, ks, grad_rows, ids=()):
    n, step = len(ks), 4
    rows = chunk_rows(n)
    whole = pl.BlockSpec((8, LANES), lambda i, s: (0, 0))
    block = lambda k: pl.BlockSpec((1, step, CAP, 1280), lambda i, s: ((s[0] + k) % NZ, i, 0, 0))
    grads = hbm(grad_rows.reshape(NZ, XC, CAP, 1280))
    out = pl.pallas_call(
        functools.partial(pack_kernel, n, step, bool(ids)),
        grid_spec=pltpu.PrefetchScalarGridSpec(
            num_scalar_prefetch=1,
            grid=(XC // step,),
            in_specs=[block(k) for k in ks] + [whole for _ in ids],
            out_specs=pl.BlockSpec((NY, step, rows, LANES), lambda i, s: (0, i, 0, 0)),
        ),
        out_shape=pltpu.HBM((NY, XC, rows, LANES), BF),
        compiler_params=params(14),
        cost_estimate=pl.CostEstimate(flops=0, bytes_accessed=700_000 * n, transcendentals=0),
        name="pack",
    )(z, *[grads] * n, *[hbm(i.reshape(8, LANES)) for i in ids])
    return out.reshape(GROUP, rows, LANES)


def read_ids(z_ref, got_ref, at, outs):
    sub = tile_iota(0)
    low = low_lanes((8, LANES))
    for q in range(GROUP // 8):
        tiles = [jnp.zeros((8, LANES), F32)] * 4
        for j in range(8):
            head = got_ref[8 * q + j, pl.ds(at, CAP), :].astype(F32)
            for t in range(4):
                row = 4 * (t // 2) + t % 2
                mine = head[row : row + 1] * 16.0 + head[row + 2 : row + 3]
                tiles[t] = jnp.where(sub == j, mine, tiles[t])
        for t, ref in enumerate(outs):
            rolled = row_roll(jnp.where(low, pltpu.roll(tiles[2 * t], 64, 1), tiles[2 * t + 1]))
            for k in range(NZ):
                ref[pl.ds(k, 1), pl.ds(q * LANES, LANES)] = diagonal(rolled, z_ref[0] + k).astype(jnp.int32)


def sums_kernel(ks, first, z_ref, *refs):
    n = len(ks)
    if first:
        got_ref, outs, ids_ref = refs[0], refs[1 : 1 + n], refs[1 + n]
        read_ids(z_ref, got_ref, (2 * n + n // 2) * CAP, refs[1 + n :])
    else:
        got_ref, ids_ref, outs = refs[0], refs[1], refs[2:]
    rows = lax.broadcasted_iota(jnp.int32, (ROWS, GROUP * CAP), 0)
    for p, k in enumerate(ks):
        pick = jnp.where(rows == ids_ref[pl.ds(k, 1), :], 1.0, 0.0).astype(BF)
        slots = jnp.concatenate(
            [
                got_ref[:, pl.ds(at * CAP, CAP), :].reshape(GROUP * CAP, LANES)
                for at in (p, n + p, 2 * n + p // 2)
            ],
            axis=1,
        )
        total = jnp.dot(pick, slots, preferred_element_type=F32)
        outs[p][pl.ds(0, ROWS), :] = total[:, :128]
        outs[p][pl.ds(ROWS, ROWS), :] = total[:, 128:256]
        last = total[:, 256:]
        outs[p][pl.ds(2 * ROWS, HALF), :] = pair(last[:HALF], last[HALF:], p % 2 == 1)


def partial_sums(z, ks, got, ids=None):
    vmem = pl.BlockSpec(memory_space=pltpu.VMEM)
    first = ids is None
    ids_shape = jax.ShapeDtypeStruct((NZ, GROUP * CAP), jnp.int32)
    outs = [jax.ShapeDtypeStruct((QROWS, LANES), F32)] * len(ks) + [ids_shape] * (2 if first else 0)
    got = pl.pallas_call(
        functools.partial(sums_kernel, ks, first),
        in_specs=[pl.BlockSpec(memory_space=pltpu.SMEM)] + [vmem] * (1 if first else 2),
        out_specs=[vmem] * len(outs),
        out_shape=outs,
        compiler_params=params(12),
        name="partial_sums",
    )(z, got, *(() if first else (ids,)))
    return dict(zip(ks, got)), tuple(got[len(ks) :])


def quarter_kernel(y_ref, *refs):
    odd = y_ref[0] % 2 == 1
    for i in range(3):
        a, b, c = (r[...] for r in refs[3 * i : 3 * i + 3])
        o_ref = refs[9 + i]
        o_ref[pl.ds(0, ROWS), :] = a
        o_ref[pl.ds(ROWS, ROWS), :] = b
        o_ref[pl.ds(2 * ROWS, HALF), :] = pair(c[:HALF], c[HALF:], odd)


def quarters(y, *arrays):
    spec = [
        pl.BlockSpec((ROWS, LANES), lambda i, s: (0, s[0])),
        pl.BlockSpec((ROWS, LANES), lambda i, s: (0, NY + s[0])),
        pl.BlockSpec((ROWS, LANES), lambda i, s: (0, 2 * NY + s[0] // 2)),
    ]
    return pl.pallas_call(
        quarter_kernel,
        grid_spec=pltpu.PrefetchScalarGridSpec(
            num_scalar_prefetch=1,
            grid=(1,),
            in_specs=spec * 3,
            out_specs=[pl.BlockSpec((QROWS, LANES), lambda i, s: (0, 0))] * 3,
        ),
        out_shape=[jax.ShapeDtypeStruct((QROWS, LANES), F32)] * 3,
        compiler_params=params(12),
        cost_estimate=pl.CostEstimate(flops=1_000_000, bytes_accessed=3_000_000, transcendentals=0),
        name="quarters",
    )(y, *[hbm(t) for t in arrays for _ in range(3)])


def fetch_kernel(ks, ids_ref, *refs):
    n = len(ks)
    tables, o_ref = refs[:n], refs[n]
    rows = lax.broadcasted_iota(jnp.int32, (GROUP * CAP, ROWS), 1).astype(F32)
    columns = jnp.transpose(ids_ref[...].astype(F32))
    low = low_lanes((GROUP, CAP, LANES))
    even = None
    for p, k in enumerate(ks):
        pick = jnp.where(rows == columns[:, k : k + 1], 1.0, 0.0).astype(BF)
        table = tables[p]
        last = table[pl.ds(2 * ROWS, HALF), :]
        moved = pltpu.roll(last.astype(F32), 64, 1).astype(BF)
        halves = [moved, last] if p % 2 else [last, moved]
        wide = jnp.concatenate(
            [table[pl.ds(0, ROWS), :], table[pl.ds(ROWS, ROWS), :], jnp.concatenate(halves, axis=0)], axis=1
        )
        found = jnp.dot(pick, wide, preferred_element_type=F32)
        found = found.astype(BF).reshape(GROUP, CAP, 3 * LANES)
        o_ref[:, pl.ds(p * CAP, CAP), :] = found[:, :, :128]
        o_ref[:, pl.ds((n + p) * CAP, CAP), :] = found[:, :, 128:256]
        if p % 2:
            o_ref[:, pl.ds((2 * n + p // 2) * CAP, CAP), :] = jnp.where(low, even, found[:, :, 256:])
        else:
            even = found[:, :, 256:]
            if p == n - 1:
                o_ref[:, pl.ds((2 * n + p // 2) * CAP, CAP), :] = even


def fetch(ks, ids, tables):
    vmem = pl.BlockSpec(memory_space=pltpu.VMEM)
    return pl.pallas_call(
        functools.partial(fetch_kernel, ks),
        in_specs=[vmem] * (1 + len(ks)),
        out_specs=vmem,
        out_shape=jax.ShapeDtypeStruct((GROUP, chunk_rows(len(ks)), LANES), BF),
        compiler_params=params(12),
        name="fetch",
    )(ids, *[tables[k] for k in ks])


def unpack_kernel(chunks, step, z_ref, *refs):
    o_ref = refs[-1]
    for ks, g_ref in zip(chunks, refs):
        n = len(ks)
        for p, k in enumerate(ks):
            z = (z_ref[0] + k) % NZ
            for u in range(step):
                for y in range(NY):
                    o_ref[z, u, :, pl.ds(y * LANES, LANES)] = g_ref[y, u, pl.ds(p * CAP, CAP), :]
                    o_ref[z, u, :, pl.ds(512 + y * LANES, LANES)] = g_ref[y, u, pl.ds((n + p) * CAP, CAP), :]
                at = pl.ds((2 * n + p // 2) * CAP, CAP)
                for t in range(2):
                    a = g_ref[2 * t, u, at, :].astype(F32)
                    b = g_ref[2 * t + 1, u, at, :].astype(F32)
                    o_ref[z, u, :, pl.ds(1024 + t * LANES, LANES)] = pair(a, b, p % 2 == 1).astype(BF)


def unpack(z, chunks, backs):
    step = 2
    out = pl.pallas_call(
        functools.partial(unpack_kernel, chunks, step),
        grid_spec=pltpu.PrefetchScalarGridSpec(
            num_scalar_prefetch=1,
            grid=(XC // step,),
            in_specs=[
                pl.BlockSpec((NY, step, chunk_rows(len(ks)), LANES), lambda i, s: (0, i, 0, 0)) for ks in chunks
            ],
            out_specs=pl.BlockSpec((NZ, step, CAP, 1280), lambda i, s: (0, i, 0, 0)),
        ),
        out_shape=pltpu.HBM((NZ, XC, CAP, 1280), BF),
        compiler_params=params(12),
        name="unpack",
    )(z, *[b.reshape(NY, XC, -1, LANES) for b in backs])
    return out.reshape(NZ * XC * CAP, 1280)


FULL_STEP = 48


def full_kernel(y_ref, *refs):
    g_refs, (w_ref, m_ref, v_ref, ow_ref, om_ref, ov_ref, all_ref) = refs[:NY], refs[NY:]
    for d in range(NY):
        all_ref[(y_ref[0] + d) % NY] = g_refs[d][...]
    for half in range(2):
        for t in range(10):
            if t < 8:
                grads = all_ref[t % NY, 2 * (t // NY) + half]
            else:
                grads = pair(all_ref[2 * (t - 8), 4], all_ref[2 * (t - 8) + 1, 4], half == 1)
            cols = pl.ds(t * LANES, LANES)
            w, m, v = adamw(w_ref[half, :, cols], m_ref[half, :, cols], v_ref[half, :, cols], grads)
            ow_ref[half, :, cols] = w
            om_ref[half, :, cols] = m
            ov_ref[half, :, cols] = v


def full_rows(y, grads, table_rows, first_moment, second_moment):
    wide = pl.BlockSpec((2, FULL_STEP, 1280), lambda i, s: (0, i, 0))
    part = pl.BlockSpec((5, FULL_STEP, LANES), lambda i, s: (0, i, 0))
    outs = pl.pallas_call(
        full_kernel,
        grid_spec=pltpu.PrefetchScalarGridSpec(
            num_scalar_prefetch=1,
            grid=(HALF // FULL_STEP,),
            in_specs=[part] * NY + [wide] * 3,
            out_specs=[wide] * 3,
            scratch_shapes=[pltpu.VMEM((NY, 5, FULL_STEP, LANES), F32)],
        ),
        out_shape=[pltpu.HBM((2, HALF, 1280), F32)] * 3,
        compiler_params=params(12),
        cost_estimate=pl.CostEstimate(flops=10_000_000, bytes_accessed=14_000_000, transcendentals=0),
        name="full_rows",
    )(
        y,
        *[g.reshape(5, HALF, LANES) for g in grads],
        *[hbm(t.reshape(2, HALF, 1280)) for t in (table_rows, first_moment, second_moment)],
    )
    return tuple(t.reshape(ROWS, 1280) for t in outs)


def along(value, axis, size, step):
    return lax.ppermute(value, axis, [(i, (i + step) % size) for i in range(size)])


def coded(x):
    root = jnp.sqrt(jnp.abs(x)) * 256.0
    return jnp.where(x < 0.0, -root, root).astype(F16)


def decoded(h):
    wide = h.astype(F32)
    return wide * jnp.abs(wide) * (1.0 / 65536.0)


def both_ways(up, down):
    up, down = lax.optimization_barrier((up, down))
    return lax.optimization_barrier((along(up, "z", NZ, 1), along(down, "z", NZ, -1)))


def send_sums(up, down):
    up, down = both_ways(coded(up), coded(down))
    return decoded(up), decoded(down)


def swap(x):
    return lax.all_to_all(x, SLAB, split_axis=0, concat_axis=0, tiled=True)


FAR, NEAR = (4, 3, 5), (2, 6, 1, 7, 0)
FIRST, LATER = (0, 1, 7, 2, 6), (3, 5, 4)


def local(table_rows, first_moment, second_moment, grad_rows, row_ids, next_ids):
    z = lax.axis_index("z").astype(jnp.int32)[None]
    y = lax.axis_index("y").astype(jnp.int32)[None]
    far = swap(pack(z, FAR, grad_rows, (row_ids, next_ids)))
    near = swap(pack(z, NEAR, grad_rows))
    mine = quarters(y, table_rows, first_moment, second_moment)
    part, (ids, wanted) = partial_sums(z, FAR, far)
    up = decoded(along(coded(part[4]), "z", NZ, 1))
    up, down = send_sums(part[3] + up, part[5])
    near, up, down = lax.optimization_barrier((near, up, down))
    part, _ = partial_sums(z, NEAR, near, ids)
    up, down = send_sums(part[2] + up, part[6] + down)
    up, down = send_sums(part[1] + up, part[7] + down)
    shared = coded(part[0] + up + down)
    summed = decoded(shared)
    own = adamw(*mine, summed)[0].astype(BF)
    grads = [shared] + [along(shared, "y", NY, -d) for d in range(1, NY)]
    tables = {0: own}
    tables[7], tables[1] = both_ways(own, own)
    tables[6], tables[2], *grads[1:] = lax.optimization_barrier(
        (along(tables[7], "z", NZ, 1), along(tables[1], "z", NZ, -1), *grads[1:])
    )
    found, tables[6], tables[2] = lax.optimization_barrier((fetch(FIRST, wanted, tables), tables[6], tables[2]))
    back = swap(found)
    tables[5], tables[3] = both_ways(tables[6], tables[2])
    tables[4] = along(tables[5], "z", NZ, 1)
    back, found = lax.optimization_barrier((back, fetch(LATER, wanted, tables)))
    backs = [back, swap(found)]
    outs = full_rows(y, [decoded(g) for g in grads], table_rows, first_moment, second_moment)
    return (*outs, unpack(z, (FIRST, LATER), backs))


def solution(mesh):
    fine = Mesh(mesh.devices.reshape(NY, NZ, 4, 2), ("y", "z", "x", "c"))
    owner = ("z", "x", "c")
    every = ("y", "z", "x", "c")
    return jax.shard_map(
        local,
        mesh=fine,
        in_specs=(P(owner, None), P(owner, None), P(owner, None), P(every, None), P(every), P(every)),
        out_specs=(P(owner, None), P(owner, None), P(owner, None), P(every, None)),
        check_vma=False,
    )
```

```python
import functools

import jax
import jax.numpy as jnp
from jax import lax
from jax.experimental import pallas as pl
from jax.experimental.pallas import tpu as pltpu
from jax.sharding import Mesh, PartitionSpec as P

STEP = 20
LANES = 128
CAP = 16
BF = jnp.bfloat16
F32 = jnp.float32
F16 = jnp.float16
SLAB = ("x", "c", "y")
GROUP = 32
NZ = 8
NY = 4
XC = 8
ROWS = 384
HALF = 192
QROWS = 960


def adamw(weights, first, second, grads):
    first_new = 0.9 * first + 0.1 * grads
    second_new = 0.95 * second + 0.05 * grads * grads
    corr_one = 1.0 - 0.9**STEP
    corr_two = 1.0 - 0.95**STEP
    update = first_new / corr_one / (jnp.sqrt(second_new / corr_two) + 1e-08) + 0.01 * weights
    return (weights - 0.1 * update, first_new, second_new)


def low_lanes(shape):
    return lax.broadcasted_iota(jnp.int32, shape, len(shape) - 1) < 64


def pair(a, b, upper):
    low = low_lanes(a.shape)
    axis = a.ndim - 1
    if isinstance(upper, bool):
        return jnp.where(low, pltpu.roll(a, 64, axis), b) if upper else jnp.where(low, a, pltpu.roll(b, 64, axis))
    return jnp.where(
        upper,
        jnp.where(low, pltpu.roll(a, 64, axis), b),
        jnp.where(low, a, pltpu.roll(b, 64, axis)),
    )


def centred(rows):
    return (rows.astype(F32) - HALF).astype(BF)


def one_hot(rows, ids):
    return jnp.where(rows == ids, jnp.ones((), BF), jnp.zeros((), BF))


def params(mib):
    return pltpu.CompilerParams(vmem_limit_bytes=mib * 1024 * 1024)


def hbm(x):
    return pltpu.with_memory_space_constraint(x, pltpu.HBM)


def tile_iota(axis):
    return lax.broadcasted_iota(jnp.int32, (8, LANES), axis)


def diagonal(rolled, shift):
    moved = pltpu.roll(rolled, (NZ * LANES - CAP * shift) % LANES, 1)
    kept = jnp.where(tile_iota(1) // CAP == tile_iota(0), moved, 0.0)
    return jnp.sum(kept, axis=0, keepdims=True)


def row_roll(x):
    return pltpu.roll(x, 0, 1, stride=CAP, stride_axis=0)


def chunk_rows(n):
    return 2 * CAP * n + CAP * ((n + 1) // 2)


def pack_kernel(n, step, with_ids, z_ref, *refs):
    blocks, o_ref = refs[:n], refs[-1]
    sub = lax.broadcasted_iota(jnp.int32, (CAP, LANES), 0)
    if with_ids:
        ids = [row_roll(r[...].astype(F32)) for r in refs[n : n + 2]]
    for u in range(step):
        rest = jnp.zeros((CAP, LANES), F32)
        if with_ids:
            for t in range(2):
                mine = diagonal(ids[t], pl.program_id(0) * step + u)
                upper = jnp.floor(mine * (1.0 / 16.0))
                lower = mine - 16.0 * upper
                for r, row in enumerate((pltpu.roll(upper, 64, 1), upper, pltpu.roll(lower, 64, 1), lower)):
                    rest = jnp.where(sub == 4 * t + r, row, rest)
        for y in range(NY):
            for p in range(n):
                o_ref[u, y, pl.ds(p * CAP, CAP), :] = blocks[p][0, u, :, pl.ds(y * LANES, LANES)]
                o_ref[u, y, pl.ds((n + p) * CAP, CAP), :] = blocks[p][0, u, :, pl.ds(512 + y * LANES, LANES)]
            cols = pl.ds(1024 + (y // 2) * LANES, LANES)
            for t in range((n + 1) // 2):
                a = blocks[2 * t][0, u, :, cols].astype(F32)
                if 2 * t + 1 < n:
                    tile = pair(a, blocks[2 * t + 1][0, u, :, cols].astype(F32), y % 2 == 1)
                else:
                    tile = jnp.where(low_lanes(a.shape), pltpu.roll(a, 64, 1) if y % 2 else a, rest)
                o_ref[u, y, pl.ds((2 * n + t) * CAP, CAP), :] = tile.astype(BF)


def pack(z, ks, grad_rows, ids=()):
    n, step = len(ks), 4
    rows = chunk_rows(n)
    whole = pl.BlockSpec((8, LANES), lambda i, s: (0, 0))
    block = lambda k: pl.BlockSpec((1, step, CAP, 1280), lambda i, s: ((s[0] + k) % NZ, i, 0, 0))
    grads = hbm(grad_rows.reshape(NZ, XC, CAP, 1280))
    out = pl.pallas_call(
        functools.partial(pack_kernel, n, step, bool(ids)),
        grid_spec=pltpu.PrefetchScalarGridSpec(
            num_scalar_prefetch=1,
            grid=(XC // step,),
            in_specs=[block(k) for k in ks] + [whole for _ in ids],
            out_specs=pl.BlockSpec((step, NY, rows, LANES), lambda i, s: (i, 0, 0, 0)),
        ),
        out_shape=pltpu.HBM((XC, NY, rows, LANES), BF),
        compiler_params=params(14),
        cost_estimate=pl.CostEstimate(flops=0, bytes_accessed=700_000 * n, transcendentals=0),
        name="pack",
    )(z, *[grads] * n, *[hbm(i.reshape(8, LANES)) for i in ids])
    return out.reshape(GROUP, rows, LANES)


def read_ids(z_ref, got_ref, at, outs):
    sub = tile_iota(0)
    low = low_lanes((8, LANES))
    for q in range(GROUP // 8):
        tiles = [jnp.zeros((8, LANES), F32)] * 4
        for j in range(8):
            head = got_ref[8 * q + j, pl.ds(at, CAP), :].astype(F32)
            for t in range(4):
                row = 4 * (t // 2) + t % 2
                mine = head[row : row + 1] * 16.0 + head[row + 2 : row + 3]
                tiles[t] = jnp.where(sub == j, mine, tiles[t])
        for t, ref in enumerate(outs):
            rolled = row_roll(jnp.where(low, pltpu.roll(tiles[2 * t], 64, 1), tiles[2 * t + 1]))
            for k in range(NZ):
                ref[pl.ds(k, 1), pl.ds(q * LANES, LANES)] = diagonal(rolled, z_ref[0] + k).astype(jnp.int32)


def sums_kernel(ks, first, z_ref, *refs):
    n = len(ks)
    if first:
        got_ref, outs, ids_ref = refs[0], refs[1 : 1 + n], refs[1 + n]
        read_ids(z_ref, got_ref, (2 * n + n // 2) * CAP, refs[1 + n :])
    else:
        got_ref, ids_ref, outs = refs[0], refs[1], refs[2:]
    rows = centred(lax.broadcasted_iota(jnp.int32, (ROWS, GROUP * CAP), 0))
    for p, k in enumerate(ks):
        pick = one_hot(rows, centred(ids_ref[pl.ds(k, 1), :]))
        slots = jnp.concatenate(
            [
                got_ref[:, pl.ds(at * CAP, CAP), :].reshape(GROUP * CAP, LANES)
                for at in (p, n + p, 2 * n + p // 2)
            ],
            axis=1,
        )
        total = jnp.dot(pick, slots, preferred_element_type=F32)
        outs[p][pl.ds(0, ROWS), :] = total[:, :128]
        outs[p][pl.ds(ROWS, ROWS), :] = total[:, 128:256]
        last = total[:, 256:]
        outs[p][pl.ds(2 * ROWS, HALF), :] = pair(last[:HALF], last[HALF:], p % 2 == 1)


def partial_sums(z, ks, got, ids=None):
    vmem = pl.BlockSpec(memory_space=pltpu.VMEM)
    first = ids is None
    ids_shape = jax.ShapeDtypeStruct((NZ, GROUP * CAP), jnp.int32)
    outs = [jax.ShapeDtypeStruct((QROWS, LANES), F32)] * len(ks) + [ids_shape] * (2 if first else 0)
    got = pl.pallas_call(
        functools.partial(sums_kernel, ks, first),
        in_specs=[pl.BlockSpec(memory_space=pltpu.SMEM)] + [vmem] * (1 if first else 2),
        out_specs=[vmem] * len(outs),
        out_shape=outs,
        compiler_params=params(12),
        name="partial_sums",
    )(z, got, *(() if first else (ids,)))
    return dict(zip(ks, got)), tuple(got[len(ks) :])


def quarter_kernel(y_ref, *refs):
    odd = y_ref[0] % 2 == 1
    for i in range(3):
        a, b, c = (r[...] for r in refs[3 * i : 3 * i + 3])
        o_ref = refs[9 + i]
        o_ref[pl.ds(0, ROWS), :] = a
        o_ref[pl.ds(ROWS, ROWS), :] = b
        o_ref[pl.ds(2 * ROWS, HALF), :] = pair(c[:HALF], c[HALF:], odd)


def quarters(y, *arrays):
    spec = [
        pl.BlockSpec((ROWS, LANES), lambda i, s: (0, s[0])),
        pl.BlockSpec((ROWS, LANES), lambda i, s: (0, NY + s[0])),
        pl.BlockSpec((ROWS, LANES), lambda i, s: (0, 2 * NY + s[0] // 2)),
    ]
    return pl.pallas_call(
        quarter_kernel,
        grid_spec=pltpu.PrefetchScalarGridSpec(
            num_scalar_prefetch=1,
            grid=(1,),
            in_specs=spec * 3,
            out_specs=[pl.BlockSpec((QROWS, LANES), lambda i, s: (0, 0))] * 3,
        ),
        out_shape=[jax.ShapeDtypeStruct((QROWS, LANES), F32)] * 3,
        compiler_params=params(12),
        cost_estimate=pl.CostEstimate(flops=1_000_000, bytes_accessed=3_000_000, transcendentals=0),
        name="quarters",
    )(y, *[hbm(t) for t in arrays for _ in range(3)])


def fetch_kernel(ks, ids_ref, *refs):
    n = len(ks)
    tables, o_ref = refs[:n], refs[n]
    rows = centred(lax.broadcasted_iota(jnp.int32, (GROUP * CAP, ROWS), 1))
    columns = jnp.transpose(ids_ref[...].astype(F32) - HALF).astype(BF)
    low = low_lanes((GROUP, CAP, LANES))
    even = None
    for p, k in enumerate(ks):
        pick = one_hot(rows, columns[:, k : k + 1])
        table = tables[p]
        last = table[pl.ds(2 * ROWS, HALF), :]
        moved = pltpu.roll(last.astype(F32), 64, 1).astype(BF)
        halves = [moved, last] if p % 2 else [last, moved]
        wide = jnp.concatenate(
            [table[pl.ds(0, ROWS), :], table[pl.ds(ROWS, ROWS), :], jnp.concatenate(halves, axis=0)], axis=1
        )
        found = jnp.dot(pick, wide, preferred_element_type=F32)
        found = found.astype(BF).reshape(GROUP, CAP, 3 * LANES)
        o_ref[:, pl.ds(p * CAP, CAP), :] = found[:, :, :128]
        o_ref[:, pl.ds((n + p) * CAP, CAP), :] = found[:, :, 128:256]
        if p % 2:
            o_ref[:, pl.ds((2 * n + p // 2) * CAP, CAP), :] = jnp.where(low, even, found[:, :, 256:])
        else:
            even = found[:, :, 256:]
            if p == n - 1:
                o_ref[:, pl.ds((2 * n + p // 2) * CAP, CAP), :] = even


def fetch(ks, ids, tables):
    vmem = pl.BlockSpec(memory_space=pltpu.VMEM)
    return pl.pallas_call(
        functools.partial(fetch_kernel, ks),
        in_specs=[vmem] * (1 + len(ks)),
        out_specs=vmem,
        out_shape=jax.ShapeDtypeStruct((GROUP, chunk_rows(len(ks)), LANES), BF),
        compiler_params=params(12),
        name="fetch",
    )(ids, *[tables[k] for k in ks])


def unpack_kernel(ks, z_ref, g_ref, *refs):
    o_ref, block_ref, sems = refs[-3:]
    n = len(ks)
    copies = []
    for p, k in enumerate(ks):
        for u in range(XC):
            rows = pl.ds(u * CAP, CAP)
            get = lambda y, at: g_ref[u * NY + y, pl.ds(at * CAP, CAP), :]
            for y in range(NY):
                block_ref[p, rows, pl.ds(y * LANES, LANES)] = get(y, p)
                block_ref[p, rows, pl.ds(512 + y * LANES, LANES)] = get(y, n + p)
            for t in range(2):
                a = get(2 * t, 2 * n + p // 2).astype(F32)
                b = get(2 * t + 1, 2 * n + p // 2).astype(F32)
                block_ref[p, rows, pl.ds(1024 + t * LANES, LANES)] = pair(a, b, p % 2 == 1).astype(BF)
        copies.append(pltpu.make_async_copy(block_ref.at[p], o_ref.at[(z_ref[0] + k) % NZ], sems.at[p]))
        copies[-1].start()
    for copy in copies:
        copy.wait()


def unpack(z, ks, back, into=None):
    n = len(ks)
    hbm_spec = pl.BlockSpec(memory_space=pltpu.HBM)
    return pl.pallas_call(
        functools.partial(unpack_kernel, ks),
        in_specs=[pl.BlockSpec(memory_space=pltpu.SMEM), pl.BlockSpec(memory_space=pltpu.VMEM)]
        + ([] if into is None else [hbm_spec]),
        out_specs=hbm_spec,
        out_shape=pltpu.HBM((NZ, XC * CAP, 1280), BF),
        input_output_aliases={} if into is None else {2: 0},
        scratch_shapes=[pltpu.VMEM((n, XC * CAP, 1280), BF), pltpu.SemaphoreType.DMA((n,))],
        compiler_params=params(8),
        cost_estimate=pl.CostEstimate(flops=0, bytes_accessed=700_000 * n, transcendentals=0),
        name="unpack",
    )(z, back, *(() if into is None else (into,)))


FULL_STEP = 48


def full_kernel(y_ref, *refs):
    g_refs, (w_ref, m_ref, v_ref, ow_ref, om_ref, ov_ref, all_ref) = refs[:NY], refs[NY:]
    for d in range(NY):
        all_ref[(y_ref[0] + d) % NY] = g_refs[d][...]
    for half in range(2):
        for t in range(10):
            if t < 8:
                grads = all_ref[t % NY, 2 * (t // NY) + half]
            else:
                grads = pair(all_ref[2 * (t - 8), 4], all_ref[2 * (t - 8) + 1, 4], half == 1)
            cols = pl.ds(t * LANES, LANES)
            w, m, v = adamw(w_ref[half, :, cols], m_ref[half, :, cols], v_ref[half, :, cols], grads)
            ow_ref[half, :, cols] = w
            om_ref[half, :, cols] = m
            ov_ref[half, :, cols] = v


def full_rows(y, grads, table_rows, first_moment, second_moment):
    wide = pl.BlockSpec((2, FULL_STEP, 1280), lambda i, s: (0, i, 0))
    part = pl.BlockSpec((5, FULL_STEP, LANES), lambda i, s: (0, i, 0))
    outs = pl.pallas_call(
        full_kernel,
        grid_spec=pltpu.PrefetchScalarGridSpec(
            num_scalar_prefetch=1,
            grid=(HALF // FULL_STEP,),
            in_specs=[part] * NY + [wide] * 3,
            out_specs=[wide] * 3,
            scratch_shapes=[pltpu.VMEM((NY, 5, FULL_STEP, LANES), F32)],
        ),
        out_shape=[pltpu.HBM((2, HALF, 1280), F32)] * 3,
        compiler_params=params(12),
        cost_estimate=pl.CostEstimate(flops=10_000_000, bytes_accessed=14_000_000, transcendentals=0),
        name="full_rows",
    )(
        y,
        *[g.reshape(5, HALF, LANES) for g in grads],
        *[hbm(t.reshape(2, HALF, 1280)) for t in (table_rows, first_moment, second_moment)],
    )
    return tuple(t.reshape(ROWS, 1280) for t in outs)


def along(value, axis, size, step):
    return lax.ppermute(value, axis, [(i, (i + step) % size) for i in range(size)])


def coded(x):
    root = jnp.sqrt(jnp.abs(x)) * 256.0
    return jnp.where(x < 0.0, -root, root).astype(F16)


def decoded(h):
    wide = h.astype(F32)
    return wide * jnp.abs(wide) * (1.0 / 65536.0)


def both_ways(up, down):
    up, down = lax.optimization_barrier((up, down))
    return lax.optimization_barrier((along(up, "z", NZ, 1), along(down, "z", NZ, -1)))


def send_sums(up, down):
    up, down = both_ways(coded(up), coded(down))
    return decoded(up), decoded(down)


def swap(x):
    return lax.all_to_all(x, SLAB, split_axis=0, concat_axis=0, tiled=True)


FAR, NEAR = (4, 3, 5), (2, 6, 1, 7, 0)
FIRST, LATER = (0, 1, 7, 2, 6), (3, 5, 4)


def local(table_rows, first_moment, second_moment, grad_rows, row_ids, next_ids):
    z = lax.axis_index("z").astype(jnp.int32)[None]
    y = lax.axis_index("y").astype(jnp.int32)[None]
    far = swap(pack(z, FAR, grad_rows, (row_ids, next_ids)))
    near = swap(pack(z, NEAR, grad_rows))
    mine = quarters(y, table_rows, first_moment, second_moment)
    part, (ids, wanted) = partial_sums(z, FAR, far)
    up = decoded(along(coded(part[4]), "z", NZ, 1))
    up, down = send_sums(part[3] + up, part[5])
    near, up, down = lax.optimization_barrier((near, up, down))
    part, _ = partial_sums(z, NEAR, near, ids)
    up, down = send_sums(part[2] + up, part[6] + down)
    up, down = send_sums(part[1] + up, part[7] + down)
    shared = coded(part[0] + up + down)
    summed = decoded(shared)
    own = adamw(*mine, summed)[0].astype(BF)
    grads = [shared] + [along(shared, "y", NY, -d) for d in range(1, NY)]
    tables = {0: own}
    tables[7], tables[1] = both_ways(own, own)
    tables[6], tables[2], *grads[1:] = lax.optimization_barrier(
        (along(tables[7], "z", NZ, 1), along(tables[1], "z", NZ, -1), *grads[1:])
    )
    found, tables[6], tables[2] = lax.optimization_barrier((fetch(FIRST, wanted, tables), tables[6], tables[2]))
    back = swap(found)
    tables[5], tables[3] = both_ways(tables[6], tables[2])
    tables[4] = along(tables[5], "z", NZ, 1)
    back, found, *grads = lax.optimization_barrier((back, fetch(LATER, wanted, tables), *grads))
    backs = [back, swap(found)]
    outs = full_rows(y, [decoded(g) for g in grads], table_rows, first_moment, second_moment)
    fetched = unpack(z, LATER, backs[1], unpack(z, FIRST, backs[0]))
    return (*outs, fetched.reshape(NZ * XC * CAP, 1280))


def solution(mesh):
    fine = Mesh(mesh.devices.reshape(NY, NZ, 4, 2), ("y", "z", "x", "c"))
    owner = ("z", "x", "c")
    every = ("y", "z", "x", "c")
    return jax.shard_map(
        local,
        mesh=fine,
        in_specs=(P(owner, None), P(owner, None), P(owner, None), P(every, None), P(every), P(every)),
        out_specs=(P(owner, None), P(owner, None), P(owner, None), P(every, None)),
        check_vma=False,
    )
```

```python
import functools

import jax
import jax.numpy as jnp
from jax import lax
from jax.experimental import pallas as pl
from jax.experimental.pallas import tpu as pltpu
from jax.sharding import Mesh, PartitionSpec as P

STEP = 20
LANES = 128
CAP = 16
BF = jnp.bfloat16
F32 = jnp.float32
F16 = jnp.float16
SLAB = ("x", "c", "y")
GROUP = 32
NZ = 8
NY = 4
XC = 8
ROWS = 384
HALF = 192
QROWS = 960


def adamw(weights, first, second, grads):
    first_new = 0.9 * first + 0.1 * grads
    second_new = 0.95 * second + 0.05 * grads * grads
    corr_one = 1.0 - 0.9**STEP
    corr_two = 1.0 - 0.95**STEP
    update = first_new / corr_one / (jnp.sqrt(second_new / corr_two) + 1e-08) + 0.01 * weights
    return (weights - 0.1 * update, first_new, second_new)


def low_lanes(shape):
    return lax.broadcasted_iota(jnp.int32, shape, len(shape) - 1) < 64


def pair(a, b, upper):
    low = low_lanes(a.shape)
    axis = a.ndim - 1
    if isinstance(upper, bool):
        return jnp.where(low, pltpu.roll(a, 64, axis), b) if upper else jnp.where(low, a, pltpu.roll(b, 64, axis))
    return jnp.where(
        upper,
        jnp.where(low, pltpu.roll(a, 64, axis), b),
        jnp.where(low, a, pltpu.roll(b, 64, axis)),
    )


def centred(rows):
    return (rows.astype(F32) - HALF).astype(BF)


def one_hot(rows, ids):
    return jnp.where(rows == ids, jnp.ones((), BF), jnp.zeros((), BF))


def params(mib):
    return pltpu.CompilerParams(vmem_limit_bytes=mib * 1024 * 1024)


def hbm(x):
    return pltpu.with_memory_space_constraint(x, pltpu.HBM)


def tile_iota(axis):
    return lax.broadcasted_iota(jnp.int32, (8, LANES), axis)


def diagonal(rolled, shift):
    moved = pltpu.roll(rolled, (NZ * LANES - CAP * shift) % LANES, 1)
    kept = jnp.where(tile_iota(1) // CAP == tile_iota(0), moved, 0.0)
    return jnp.sum(kept, axis=0, keepdims=True)


def row_roll(x):
    return pltpu.roll(x, 0, 1, stride=CAP, stride_axis=0)


def chunk_rows(n):
    return 2 * CAP * n + CAP * ((n + 1) // 2)


def pack_kernel(n, step, with_ids, z_ref, *refs):
    blocks, o_ref = refs[:n], refs[-1]
    sub = lax.broadcasted_iota(jnp.int32, (CAP, LANES), 0)
    if with_ids:
        ids = [row_roll(r[...].astype(F32)) for r in refs[n : n + 2]]
    for u in range(step):
        rest = jnp.zeros((CAP, LANES), F32)
        if with_ids:
            for t in range(2):
                mine = diagonal(ids[t], pl.program_id(0) * step + u)
                upper = jnp.floor(mine * (1.0 / 16.0))
                lower = mine - 16.0 * upper
                for r, row in enumerate((pltpu.roll(upper, 64, 1), upper, pltpu.roll(lower, 64, 1), lower)):
                    rest = jnp.where(sub == 4 * t + r, row, rest)
        for y in range(NY):
            for p in range(n):
                o_ref[u, y, pl.ds(p * CAP, CAP), :] = blocks[p][0, u, :, pl.ds(y * LANES, LANES)]
                o_ref[u, y, pl.ds((n + p) * CAP, CAP), :] = blocks[p][0, u, :, pl.ds(512 + y * LANES, LANES)]
            cols = pl.ds(1024 + (y // 2) * LANES, LANES)
            for t in range((n + 1) // 2):
                a = blocks[2 * t][0, u, :, cols].astype(F32)
                if 2 * t + 1 < n:
                    tile = pair(a, blocks[2 * t + 1][0, u, :, cols].astype(F32), y % 2 == 1)
                else:
                    tile = jnp.where(low_lanes(a.shape), pltpu.roll(a, 64, 1) if y % 2 else a, rest)
                o_ref[u, y, pl.ds((2 * n + t) * CAP, CAP), :] = tile.astype(BF)


def pack(z, ks, grad_rows, ids=()):
    n, step = len(ks), 4
    rows = chunk_rows(n)
    whole = pl.BlockSpec((8, LANES), lambda i, s: (0, 0))
    block = lambda k: pl.BlockSpec((1, step, CAP, 1280), lambda i, s: ((s[0] + k) % NZ, i, 0, 0))
    grads = hbm(grad_rows.reshape(NZ, XC, CAP, 1280))
    out = pl.pallas_call(
        functools.partial(pack_kernel, n, step, bool(ids)),
        grid_spec=pltpu.PrefetchScalarGridSpec(
            num_scalar_prefetch=1,
            grid=(XC // step,),
            in_specs=[block(k) for k in ks] + [whole for _ in ids],
            out_specs=pl.BlockSpec((step, NY, rows, LANES), lambda i, s: (i, 0, 0, 0)),
        ),
        out_shape=pltpu.HBM((XC, NY, rows, LANES), BF),
        compiler_params=params(14),
        cost_estimate=pl.CostEstimate(flops=0, bytes_accessed=700_000 * n, transcendentals=0),
        name="pack",
    )(z, *[grads] * n, *[hbm(i.reshape(8, LANES)) for i in ids])
    return out.reshape(GROUP, rows, LANES)


def read_ids(z_ref, got_ref, at, outs):
    sub = tile_iota(0)
    low = low_lanes((8, LANES))
    for q in range(GROUP // 8):
        tiles = [jnp.zeros((8, LANES), F32)] * 4
        for j in range(8):
            head = got_ref[8 * q + j, pl.ds(at, CAP), :].astype(F32)
            for t in range(4):
                row = 4 * (t // 2) + t % 2
                mine = head[row : row + 1] * 16.0 + head[row + 2 : row + 3]
                tiles[t] = jnp.where(sub == j, mine, tiles[t])
        for t, ref in enumerate(outs):
            rolled = row_roll(jnp.where(low, pltpu.roll(tiles[2 * t], 64, 1), tiles[2 * t + 1]))
            for k in range(NZ):
                ref[pl.ds(k, 1), pl.ds(q * LANES, LANES)] = diagonal(rolled, z_ref[0] + k).astype(jnp.int32)


def sums_kernel(ks, first, wanted, z_ref, *refs):
    n = len(ks)
    if first:
        got_ref, outs, ids_ref = refs[0], refs[1 : 1 + n], refs[1 + n]
        read_ids(z_ref, got_ref, (2 * n + n // 2) * CAP, refs[1 + n :])
    else:
        got_ref, ids_ref, outs = refs[0], refs[1], refs[2:]
    rows = centred(lax.broadcasted_iota(jnp.int32, (ROWS, GROUP * CAP), 0))
    for out_ref, k in zip(outs, wanted):
        p = ks.index(k)
        pick = one_hot(rows, centred(ids_ref[pl.ds(k, 1), :]))
        slots = jnp.concatenate(
            [
                got_ref[:, pl.ds(at * CAP, CAP), :].reshape(GROUP * CAP, LANES)
                for at in (p, n + p, 2 * n + p // 2)
            ],
            axis=1,
        )
        total = jnp.dot(pick, slots, preferred_element_type=F32)
        out_ref[pl.ds(0, ROWS), :] = total[:, :128]
        out_ref[pl.ds(ROWS, ROWS), :] = total[:, 128:256]
        last = total[:, 256:]
        out_ref[pl.ds(2 * ROWS, HALF), :] = pair(last[:HALF], last[HALF:], p % 2 == 1)


def partial_sums(z, ks, got, ids=None, wanted=None):
    vmem = pl.BlockSpec(memory_space=pltpu.VMEM)
    first = ids is None
    wanted = wanted or ks
    ids_shape = jax.ShapeDtypeStruct((NZ, GROUP * CAP), jnp.int32)
    outs = [jax.ShapeDtypeStruct((QROWS, LANES), F32)] * len(wanted) + [ids_shape] * (2 if first else 0)
    got = pl.pallas_call(
        functools.partial(sums_kernel, ks, first, wanted),
        in_specs=[pl.BlockSpec(memory_space=pltpu.SMEM)] + [vmem] * (1 if first else 2),
        out_specs=[vmem] * len(outs),
        out_shape=outs,
        compiler_params=params(12),
        name="partial_sums",
    )(z, got, *(() if first else (ids,)))
    sums = dict(zip(wanted, got))
    return (sums, tuple(got[len(ks) :])) if first else sums


def quarter_kernel(y_ref, *refs):
    odd = y_ref[0] % 2 == 1
    for i in range(3):
        a, b, c = (r[...] for r in refs[3 * i : 3 * i + 3])
        o_ref = refs[9 + i]
        o_ref[pl.ds(0, ROWS), :] = a
        o_ref[pl.ds(ROWS, ROWS), :] = b
        o_ref[pl.ds(2 * ROWS, HALF), :] = pair(c[:HALF], c[HALF:], odd)


def quarters(y, *arrays):
    spec = [
        pl.BlockSpec((ROWS, LANES), lambda i, s: (0, s[0])),
        pl.BlockSpec((ROWS, LANES), lambda i, s: (0, NY + s[0])),
        pl.BlockSpec((ROWS, LANES), lambda i, s: (0, 2 * NY + s[0] // 2)),
    ]
    return pl.pallas_call(
        quarter_kernel,
        grid_spec=pltpu.PrefetchScalarGridSpec(
            num_scalar_prefetch=1,
            grid=(1,),
            in_specs=spec * 3,
            out_specs=[pl.BlockSpec((QROWS, LANES), lambda i, s: (0, 0))] * 3,
        ),
        out_shape=[jax.ShapeDtypeStruct((QROWS, LANES), F32)] * 3,
        compiler_params=params(12),
        cost_estimate=pl.CostEstimate(flops=1_000_000, bytes_accessed=3_000_000, transcendentals=0),
        name="quarters",
    )(y, *[hbm(t) for t in arrays for _ in range(3)])


def back_rows(ks):
    return chunk_rows(len(ks)) - (CAP if ks == FIRST else 0)


def fetch_kernel(ks, some, ids_ref, *refs):
    n = len(ks)
    tables, (out_ref, o_ref, sems) = refs[: len(some)], refs[-3:]
    rows = centred(lax.broadcasted_iota(jnp.int32, (GROUP * CAP, ROWS), 1))
    columns = jnp.transpose(ids_ref[...].astype(F32) - HALF).astype(BF)
    low = low_lanes((GROUP, CAP, LANES))
    even = rest = None
    copies = []

    def leave(at, value):
        piece = (slice(None), pl.ds(at * CAP, CAP))
        o_ref[piece] = value
        copies.append(pltpu.make_async_copy(o_ref.at[piece], out_ref.at[piece], sems.at[at]))
        copies[-1].start()

    def find(k, wide):
        found = jnp.dot(one_hot(rows, columns[:, k : k + 1]), wide, preferred_element_type=F32)
        return found.astype(BF).reshape(GROUP, CAP, wide.shape[1])

    for table, k in zip(tables, some):
        p = ks.index(k) if k in ks else -1
        last = table[pl.ds(2 * ROWS, HALF), :]
        moved = pltpu.roll(last.astype(F32), 64, 1).astype(BF)
        ends = jnp.concatenate([moved, last] if p % 2 else [last, moved], axis=0)
        if p < 0:
            rest = find(k, ends)
            continue
        found = find(k, jnp.concatenate([table[pl.ds(0, ROWS), :], table[pl.ds(ROWS, ROWS), :], ends], axis=1))
        leave(p, found[:, :, :128])
        leave(n + p, found[:, :, 128:256])
        if p % 2:
            leave(2 * n + p // 2, jnp.where(low, even, found[:, :, 256:]))
        elif p < n - 1:
            even = found[:, :, 256:]
        elif rest is not None:
            leave(2 * n + p // 2, jnp.where(low, found[:, :, 256:], rest))
    for copy in copies:
        copy.wait()


def fetch(ks, some, ids, tables, into=None):
    vmem = pl.BlockSpec(memory_space=pltpu.VMEM)
    hbm_spec = pl.BlockSpec(memory_space=pltpu.HBM)
    shape = (GROUP, back_rows(ks), LANES)
    return pl.pallas_call(
        functools.partial(fetch_kernel, ks, some),
        in_specs=[vmem] * (1 + len(some)) + ([] if into is None else [hbm_spec]),
        out_specs=hbm_spec,
        out_shape=pltpu.HBM(shape, BF),
        input_output_aliases={} if into is None else {1 + len(some): 0},
        scratch_shapes=[pltpu.VMEM(shape, BF), pltpu.SemaphoreType.DMA((shape[1] // CAP,))],
        compiler_params=params(12),
        name="fetch",
    )(ids, *[tables[k] for k in some], *(() if into is None else (into,)))


def unpack_kernel(ks, z_ref, g_ref, *refs):
    o_ref, block_ref, sems = refs[-3:]
    n = len(ks)
    copies = []

    def last_columns(slot, p, odd):
        for u in range(XC):
            get = lambda y: g_ref[u * NY + y, pl.ds((2 * n + p // 2) * CAP, CAP), :].astype(F32)
            for t in range(2):
                block_ref[slot, pl.ds(u * CAP, CAP), pl.ds(1024 + t * LANES, LANES)] = pair(
                    get(2 * t), get(2 * t + 1), odd
                ).astype(BF)

    def leave(slot, k, cols):
        piece = (slice(None), cols)
        copies.append(
            pltpu.make_async_copy(
                block_ref.at[slot].at[piece], o_ref.at[(z_ref[0] + k) % NZ].at[piece], sems.at[slot]
            )
        )
        copies[-1].start()

    for p, k in enumerate(ks):
        for u in range(XC):
            rows = pl.ds(u * CAP, CAP)
            for y in range(NY):
                block_ref[p, rows, pl.ds(y * LANES, LANES)] = g_ref[u * NY + y, pl.ds(p * CAP, CAP), :]
                block_ref[p, rows, pl.ds(512 + y * LANES, LANES)] = g_ref[u * NY + y, pl.ds((n + p) * CAP, CAP), :]
        if ks == FIRST and p == n - 1:
            leave(p, k, pl.ds(0, 1024))
        else:
            last_columns(p, p, p % 2 == 1)
            leave(p, k, pl.ds(0, 1280))
    if ks == LATER:
        last_columns(n, n - 1, True)
        leave(n, FIRST[-1], pl.ds(1024, 256))
    for copy in copies:
        copy.wait()


def unpack(z, ks, back, into=None):
    n = len(ks) + (ks == LATER)
    hbm_spec = pl.BlockSpec(memory_space=pltpu.HBM)
    return pl.pallas_call(
        functools.partial(unpack_kernel, ks),
        in_specs=[pl.BlockSpec(memory_space=pltpu.SMEM), pl.BlockSpec(memory_space=pltpu.VMEM)]
        + ([] if into is None else [hbm_spec]),
        out_specs=hbm_spec,
        out_shape=pltpu.HBM((NZ, XC * CAP, 1280), BF),
        input_output_aliases={} if into is None else {2: 0},
        scratch_shapes=[pltpu.VMEM((n, XC * CAP, 1280), BF), pltpu.SemaphoreType.DMA((n,))],
        compiler_params=params(8),
        cost_estimate=pl.CostEstimate(flops=0, bytes_accessed=700_000 * n, transcendentals=0),
        name="unpack",
    )(z, back, *(() if into is None else (into,)))


FULL_STEP = 48


def full_kernel(y_ref, *refs):
    g_refs, (w_ref, m_ref, v_ref, ow_ref, om_ref, ov_ref, all_ref) = refs[:NY], refs[NY:]
    for d in range(NY):
        all_ref[(y_ref[0] + d) % NY] = g_refs[d][...]
    for half in range(2):
        for t in range(10):
            if t < 8:
                grads = all_ref[t % NY, 2 * (t // NY) + half]
            else:
                grads = pair(all_ref[2 * (t - 8), 4], all_ref[2 * (t - 8) + 1, 4], half == 1)
            cols = pl.ds(t * LANES, LANES)
            w, m, v = adamw(w_ref[half, :, cols], m_ref[half, :, cols], v_ref[half, :, cols], grads)
            ow_ref[half, :, cols] = w
            om_ref[half, :, cols] = m
            ov_ref[half, :, cols] = v


def full_rows(y, grads, table_rows, first_moment, second_moment):
    wide = pl.BlockSpec((2, FULL_STEP, 1280), lambda i, s: (0, i, 0))
    part = pl.BlockSpec((5, FULL_STEP, LANES), lambda i, s: (0, i, 0))
    outs = pl.pallas_call(
        full_kernel,
        grid_spec=pltpu.PrefetchScalarGridSpec(
            num_scalar_prefetch=1,
            grid=(HALF // FULL_STEP,),
            in_specs=[part] * NY + [wide] * 3,
            out_specs=[wide] * 3,
            scratch_shapes=[pltpu.VMEM((NY, 5, FULL_STEP, LANES), F32)],
        ),
        out_shape=[pltpu.HBM((2, HALF, 1280), F32)] * 3,
        compiler_params=params(12),
        cost_estimate=pl.CostEstimate(flops=10_000_000, bytes_accessed=14_000_000, transcendentals=0),
        name="full_rows",
    )(
        y,
        *[g.reshape(5, HALF, LANES) for g in grads],
        *[hbm(t.reshape(2, HALF, 1280)) for t in (table_rows, first_moment, second_moment)],
    )
    return tuple(t.reshape(ROWS, 1280) for t in outs)


def along(value, axis, size, step):
    return lax.ppermute(value, axis, [(i, (i + step) % size) for i in range(size)])


def coded(x):
    root = jnp.sqrt(jnp.abs(x)) * 256.0
    return jnp.where(x < 0.0, -root, root).astype(F16)


def decoded(h):
    wide = h.astype(F32)
    return wide * jnp.abs(wide) * (1.0 / 65536.0)


def both_ways(up, down):
    up, down = lax.optimization_barrier((up, down))
    return lax.optimization_barrier((along(up, "z", NZ, 1), along(down, "z", NZ, -1)))


def send_sums(up, down):
    up, down = along(coded(up), "z", NZ, 1), along(coded(down), "z", NZ, -1)
    up, down = lax.optimization_barrier((up, down))
    return decoded(up), decoded(down)


def swap(x):
    return lax.all_to_all(x, SLAB, split_axis=0, concat_axis=0, tiled=True)


FAR, NEAR = (4, 3, 5), (2, 6, 1, 7, 0)
FIRST, LATER = (0, 1, 2, 6, 7), (3, 5, 4)


def local(table_rows, first_moment, second_moment, grad_rows, row_ids, next_ids):
    z = lax.axis_index("z").astype(jnp.int32)[None]
    y = lax.axis_index("y").astype(jnp.int32)[None]
    far = swap(pack(z, FAR, grad_rows, (row_ids, next_ids)))
    near = swap(pack(z, NEAR, grad_rows))
    mine = quarters(y, table_rows, first_moment, second_moment)
    part, (ids, wanted) = partial_sums(z, FAR, far)
    up = decoded(along(coded(part[4]), "z", NZ, 1))
    up, down = send_sums(part[3] + up, part[5])
    near, up, down = lax.optimization_barrier((near, up, down))
    part = partial_sums(z, NEAR, near, ids, (2, 6))
    up, down = send_sums(part[2] + up, part[6] + down)
    part = partial_sums(z, NEAR, near, ids, (1, 7, 0))
    up, down = send_sums(part[1] + up, part[7] + down)
    shared = coded(part[0] + up + down)
    summed = decoded(shared)
    own = adamw(*mine, summed)[0].astype(BF)
    grads = [shared] + [along(shared, "y", NY, -d) for d in range(1, NY)]
    tables = {0: own}
    tables[7], tables[1] = both_ways(own, own)
    found = fetch(FIRST, (0, 1, 7), wanted, tables)
    tables[6], tables[2], *grads[1:] = lax.optimization_barrier(
        (along(tables[7], "z", NZ, 1), along(tables[1], "z", NZ, -1), *grads[1:])
    )
    found = fetch(FIRST, (2, 6), wanted, tables, found)
    found, tables[6], tables[2] = lax.optimization_barrier((found, tables[6], tables[2]))
    back = swap(found)
    tables[5], tables[3] = both_ways(tables[6], tables[2])
    tables[4] = along(tables[5], "z", NZ, 1)
    back, found, *grads = lax.optimization_barrier((back, fetch(LATER, (7, *LATER), wanted, tables), *grads))
    backs = [back, swap(found)]
    outs = full_rows(y, [decoded(g) for g in grads], table_rows, first_moment, second_moment)
    fetched = unpack(z, LATER, backs[1], unpack(z, FIRST, backs[0]))
    return (*outs, fetched.reshape(NZ * XC * CAP, 1280))


def solution(mesh):
    fine = Mesh(mesh.devices.reshape(NY, NZ, 4, 2), ("y", "z", "x", "c"))
    owner = ("z", "x", "c")
    every = ("y", "z", "x", "c")
    return jax.shard_map(
        local,
        mesh=fine,
        in_specs=(P(owner, None), P(owner, None), P(owner, None), P(every, None), P(every), P(every)),
        out_specs=(P(owner, None), P(owner, None), P(owner, None), P(every, None)),
        check_vma=False,
    )
```

```python
import functools

import jax
import jax.numpy as jnp
from jax import lax
from jax.experimental import pallas as pl
from jax.experimental.pallas import tpu as pltpu
from jax.sharding import Mesh, PartitionSpec as P

STEP = 20
LANES = 128
CAP = 16
BF = jnp.bfloat16
F32 = jnp.float32
F16 = jnp.float16
SLAB = ("x", "c", "y")
GROUP = 32
NZ = 8
NY = 4
XC = 8
ROWS = 384
HALF = 192
QROWS = 960


def adamw(weights, first, second, grads):
    first_new = 0.9 * first + 0.1 * grads
    second_new = 0.95 * second + 0.05 * grads * grads
    corr_one = 1.0 - 0.9**STEP
    corr_two = 1.0 - 0.95**STEP
    update = first_new / corr_one / (jnp.sqrt(second_new / corr_two) + 1e-08) + 0.01 * weights
    return (weights - 0.1 * update, first_new, second_new)


def low_lanes(shape):
    return lax.broadcasted_iota(jnp.int32, shape, len(shape) - 1) < 64


def pair(a, b, upper):
    low = low_lanes(a.shape)
    axis = a.ndim - 1
    if isinstance(upper, bool):
        return jnp.where(low, pltpu.roll(a, 64, axis), b) if upper else jnp.where(low, a, pltpu.roll(b, 64, axis))
    return jnp.where(
        upper,
        jnp.where(low, pltpu.roll(a, 64, axis), b),
        jnp.where(low, a, pltpu.roll(b, 64, axis)),
    )


def centred(rows):
    return (rows.astype(F32) - HALF).astype(BF)


def one_hot(rows, ids):
    return jnp.where(rows == ids, jnp.ones((), BF), jnp.zeros((), BF))


def params(mib):
    return pltpu.CompilerParams(vmem_limit_bytes=mib * 1024 * 1024)


def hbm(x):
    return pltpu.with_memory_space_constraint(x, pltpu.HBM)


def tile_iota(axis):
    return lax.broadcasted_iota(jnp.int32, (8, LANES), axis)


def diagonal(rolled, shift):
    moved = pltpu.roll(rolled, (NZ * LANES - CAP * shift) % LANES, 1)
    kept = jnp.where(tile_iota(1) // CAP == tile_iota(0), moved, 0.0)
    return jnp.sum(kept, axis=0, keepdims=True)


def row_roll(x):
    return pltpu.roll(x, 0, 1, stride=CAP, stride_axis=0)


def chunk_rows(n):
    return 2 * CAP * n + CAP * ((n + 1) // 2)


def pack_kernel(n, step, with_ids, z_ref, *refs):
    blocks, o_ref = refs[:n], refs[-1]
    sub = lax.broadcasted_iota(jnp.int32, (CAP, LANES), 0)
    if with_ids:
        ids = [row_roll(r[...].astype(F32)) for r in refs[n : n + 2]]
    for u in range(step):
        rest = jnp.zeros((CAP, LANES), F32)
        if with_ids:
            for t in range(2):
                mine = diagonal(ids[t], pl.program_id(0) * step + u)
                upper = jnp.floor(mine * (1.0 / 16.0))
                lower = mine - 16.0 * upper
                for r, row in enumerate((pltpu.roll(upper, 64, 1), upper, pltpu.roll(lower, 64, 1), lower)):
                    rest = jnp.where(sub == 4 * t + r, row, rest)
        for y in range(NY):
            for p in range(n):
                o_ref[u, y, pl.ds(p * CAP, CAP), :] = blocks[p][0, u, :, pl.ds(y * LANES, LANES)]
                o_ref[u, y, pl.ds((n + p) * CAP, CAP), :] = blocks[p][0, u, :, pl.ds(512 + y * LANES, LANES)]
            cols = pl.ds(1024 + (y // 2) * LANES, LANES)
            for t in range((n + 1) // 2):
                a = blocks[2 * t][0, u, :, cols].astype(F32)
                if 2 * t + 1 < n:
                    tile = pair(a, blocks[2 * t + 1][0, u, :, cols].astype(F32), y % 2 == 1)
                else:
                    tile = jnp.where(low_lanes(a.shape), pltpu.roll(a, 64, 1) if y % 2 else a, rest)
                o_ref[u, y, pl.ds((2 * n + t) * CAP, CAP), :] = tile.astype(BF)


def pack(z, ks, grad_rows, ids=()):
    n, step = len(ks), 4
    rows = chunk_rows(n)
    whole = pl.BlockSpec((8, LANES), lambda i, s: (0, 0))
    block = lambda k: pl.BlockSpec((1, step, CAP, 1280), lambda i, s: ((s[0] + k) % NZ, i, 0, 0))
    grads = hbm(grad_rows.reshape(NZ, XC, CAP, 1280))
    out = pl.pallas_call(
        functools.partial(pack_kernel, n, step, bool(ids)),
        grid_spec=pltpu.PrefetchScalarGridSpec(
            num_scalar_prefetch=1,
            grid=(XC // step,),
            in_specs=[block(k) for k in ks] + [whole for _ in ids],
            out_specs=pl.BlockSpec((step, NY, rows, LANES), lambda i, s: (i, 0, 0, 0)),
        ),
        out_shape=pltpu.HBM((XC, NY, rows, LANES), BF),
        compiler_params=params(14),
        cost_estimate=pl.CostEstimate(flops=0, bytes_accessed=700_000 * n, transcendentals=0),
        name="pack",
    )(z, *[grads] * n, *[hbm(i.reshape(8, LANES)) for i in ids])
    return out.reshape(GROUP, rows, LANES)


def pack_far_kernel(z_ref, row_ref, next_ref, g_ref, out_ref, ids_ref, block_ref, o_ref, in_sems, sems):
    n = len(FAR)
    loads = [pltpu.make_async_copy(r, ids_ref.at[t], in_sems.at[n + t]) for t, r in enumerate((row_ref, next_ref))]
    for p, k in enumerate(FAR):
        loads.append(pltpu.make_async_copy(g_ref.at[(z_ref[0] + k) % NZ], block_ref.at[p], in_sems.at[p]))
    for load in loads:
        load.start()
    copies = []

    def leave(at):
        piece = (slice(None), slice(None), pl.ds(at * CAP, CAP))
        copies.append(pltpu.make_async_copy(o_ref.at[piece], out_ref.at[piece], sems.at[at]))
        copies[-1].start()

    sub = lax.broadcasted_iota(jnp.int32, (CAP, LANES), 0)
    rests = [jnp.zeros((CAP, LANES), F32)] * XC
    for t in range(2):
        loads[t].wait()
        ids = row_roll(ids_ref[t].astype(F32))
        for u in range(XC):
            mine = diagonal(ids, u)
            upper = jnp.floor(mine * (1.0 / 16.0))
            lower = mine - 16.0 * upper
            for r, row in enumerate((pltpu.roll(upper, 64, 1), upper, pltpu.roll(lower, 64, 1), lower)):
                rests[u] = jnp.where(sub == 4 * t + r, row, rests[u])
    low = low_lanes((CAP, LANES))
    for p in range(n):
        loads[2 + p].wait()
        for u in range(XC):
            rows = pl.ds(u * CAP, CAP)
            for y in range(NY):
                o_ref[u, y, pl.ds(p * CAP, CAP), :] = block_ref[p, rows, pl.ds(y * LANES, LANES)]
                o_ref[u, y, pl.ds((n + p) * CAP, CAP), :] = block_ref[p, rows, pl.ds(512 + y * LANES, LANES)]
                if p % 2 == 0 and p < n - 1:
                    continue
                cols = pl.ds(1024 + (y // 2) * LANES, LANES)
                b = block_ref[p, rows, cols].astype(F32)
                if p % 2:
                    tile = pair(block_ref[p - 1, rows, cols].astype(F32), b, y % 2 == 1)
                else:
                    tile = jnp.where(low, pltpu.roll(b, 64, 1) if y % 2 else b, rests[u])
                o_ref[u, y, pl.ds((2 * n + p // 2) * CAP, CAP), :] = tile.astype(BF)
        leave(p)
        leave(n + p)
        if p % 2 or p == n - 1:
            leave(2 * n + p // 2)
    for copy in copies:
        copy.wait()


def pack_far(z, grad_rows, row_ids, next_ids):
    n = len(FAR)
    hbm_spec = pl.BlockSpec(memory_space=pltpu.HBM)
    shape = (XC, NY, chunk_rows(n), LANES)
    out = pl.pallas_call(
        pack_far_kernel,
        in_specs=[pl.BlockSpec(memory_space=pltpu.SMEM)] + [hbm_spec] * 3,
        out_specs=hbm_spec,
        out_shape=pltpu.HBM(shape, BF),
        scratch_shapes=[
            pltpu.VMEM((2, 8, LANES), jnp.int32),
            pltpu.VMEM((n, XC * CAP, 1280), BF),
            pltpu.VMEM(shape, BF),
            pltpu.SemaphoreType.DMA((n + 2,)),
            pltpu.SemaphoreType.DMA((shape[2] // CAP,)),
        ],
        compiler_params=params(8),
        name="pack_far",
    )(
        z,
        hbm(row_ids.reshape(8, LANES)),
        hbm(next_ids.reshape(8, LANES)),
        hbm(grad_rows.reshape(NZ, XC * CAP, 1280)),
    )
    return out.reshape(GROUP, shape[2], LANES)


def read_ids(z_ref, got_ref, at, outs):
    sub = tile_iota(0)
    low = low_lanes((8, LANES))
    for q in range(GROUP // 8):
        tiles = [jnp.zeros((8, LANES), F32)] * 4
        for j in range(8):
            head = got_ref[8 * q + j, pl.ds(at, CAP), :].astype(F32)
            for t in range(4):
                row = 4 * (t // 2) + t % 2
                mine = head[row : row + 1] * 16.0 + head[row + 2 : row + 3]
                tiles[t] = jnp.where(sub == j, mine, tiles[t])
        for t, ref in enumerate(outs):
            rolled = row_roll(jnp.where(low, pltpu.roll(tiles[2 * t], 64, 1), tiles[2 * t + 1]))
            for k in range(NZ):
                ref[pl.ds(k, 1), pl.ds(q * LANES, LANES)] = diagonal(rolled, z_ref[0] + k).astype(jnp.int32)


def sums_kernel(ks, first, wanted, z_ref, *refs):
    n = len(ks)
    if first:
        got_ref, outs, ids_ref = refs[0], refs[1 : 1 + n], refs[1 + n]
        read_ids(z_ref, got_ref, (2 * n + n // 2) * CAP, refs[1 + n :])
    else:
        got_ref, ids_ref, outs = refs[0], refs[1], refs[2:]
    rows = centred(lax.broadcasted_iota(jnp.int32, (ROWS, GROUP * CAP), 0))
    for out_ref, k in zip(outs, wanted):
        p = ks.index(k)
        pick = one_hot(rows, centred(ids_ref[pl.ds(k, 1), :]))
        slots = jnp.concatenate(
            [
                got_ref[:, pl.ds(at * CAP, CAP), :].reshape(GROUP * CAP, LANES)
                for at in (p, n + p, 2 * n + p // 2)
            ],
            axis=1,
        )
        total = jnp.dot(pick, slots, preferred_element_type=F32)
        out_ref[pl.ds(0, ROWS), :] = total[:, :128]
        out_ref[pl.ds(ROWS, ROWS), :] = total[:, 128:256]
        last = total[:, 256:]
        out_ref[pl.ds(2 * ROWS, HALF), :] = pair(last[:HALF], last[HALF:], p % 2 == 1)


def partial_sums(z, ks, got, ids=None, wanted=None):
    vmem = pl.BlockSpec(memory_space=pltpu.VMEM)
    first = ids is None
    wanted = wanted or ks
    ids_shape = jax.ShapeDtypeStruct((NZ, GROUP * CAP), jnp.int32)
    outs = [jax.ShapeDtypeStruct((QROWS, LANES), F32)] * len(wanted) + [ids_shape] * (2 if first else 0)
    got = pl.pallas_call(
        functools.partial(sums_kernel, ks, first, wanted),
        in_specs=[pl.BlockSpec(memory_space=pltpu.SMEM)] + [vmem] * (1 if first else 2),
        out_specs=[vmem] * len(outs),
        out_shape=outs,
        compiler_params=params(12),
        name="partial_sums",
    )(z, got, *(() if first else (ids,)))
    sums = dict(zip(wanted, got))
    return (sums, tuple(got[len(ks) :])) if first else sums


def quarter_kernel(y_ref, *refs):
    odd = y_ref[0] % 2 == 1
    for i in range(3):
        a, b, c = (r[...] for r in refs[3 * i : 3 * i + 3])
        o_ref = refs[9 + i]
        o_ref[pl.ds(0, ROWS), :] = a
        o_ref[pl.ds(ROWS, ROWS), :] = b
        o_ref[pl.ds(2 * ROWS, HALF), :] = pair(c[:HALF], c[HALF:], odd)


def quarters(y, *arrays):
    spec = [
        pl.BlockSpec((ROWS, LANES), lambda i, s: (0, s[0])),
        pl.BlockSpec((ROWS, LANES), lambda i, s: (0, NY + s[0])),
        pl.BlockSpec((ROWS, LANES), lambda i, s: (0, 2 * NY + s[0] // 2)),
    ]
    return pl.pallas_call(
        quarter_kernel,
        grid_spec=pltpu.PrefetchScalarGridSpec(
            num_scalar_prefetch=1,
            grid=(1,),
            in_specs=spec * 3,
            out_specs=[pl.BlockSpec((QROWS, LANES), lambda i, s: (0, 0))] * 3,
        ),
        out_shape=[jax.ShapeDtypeStruct((QROWS, LANES), F32)] * 3,
        compiler_params=params(12),
        cost_estimate=pl.CostEstimate(flops=1_000_000, bytes_accessed=3_000_000, transcendentals=0),
        name="quarters",
    )(y, *[hbm(t) for t in arrays for _ in range(3)])


def back_rows(ks):
    return chunk_rows(len(ks)) - (CAP if ks == FIRST else 0)


def fetch_kernel(ks, some, ids_ref, *refs):
    n = len(ks)
    tables, (out_ref, o_ref, sems) = refs[: len(some)], refs[-3:]
    rows = centred(lax.broadcasted_iota(jnp.int32, (GROUP * CAP, ROWS), 1))
    columns = jnp.transpose(ids_ref[...].astype(F32) - HALF).astype(BF)
    low = low_lanes((GROUP, CAP, LANES))
    even = rest = None
    copies = []

    def leave(at, value):
        piece = (slice(None), pl.ds(at * CAP, CAP))
        o_ref[piece] = value
        copies.append(pltpu.make_async_copy(o_ref.at[piece], out_ref.at[piece], sems.at[at]))
        copies[-1].start()

    def find(k, wide):
        found = jnp.dot(one_hot(rows, columns[:, k : k + 1]), wide, preferred_element_type=F32)
        return found.astype(BF).reshape(GROUP, CAP, wide.shape[1])

    for table, k in zip(tables, some):
        p = ks.index(k) if k in ks else -1
        last = table[pl.ds(2 * ROWS, HALF), :]
        moved = pltpu.roll(last.astype(F32), 64, 1).astype(BF)
        ends = jnp.concatenate([moved, last] if p % 2 else [last, moved], axis=0)
        if p < 0:
            rest = find(k, ends)
            continue
        found = find(k, jnp.concatenate([table[pl.ds(0, ROWS), :], table[pl.ds(ROWS, ROWS), :], ends], axis=1))
        leave(p, found[:, :, :128])
        leave(n + p, found[:, :, 128:256])
        if p % 2:
            leave(2 * n + p // 2, jnp.where(low, even, found[:, :, 256:]))
        elif p < n - 1:
            even = found[:, :, 256:]
        elif rest is not None:
            leave(2 * n + p // 2, jnp.where(low, found[:, :, 256:], rest))
    for copy in copies:
        copy.wait()


def fetch(ks, some, ids, tables, into=None):
    vmem = pl.BlockSpec(memory_space=pltpu.VMEM)
    hbm_spec = pl.BlockSpec(memory_space=pltpu.HBM)
    shape = (GROUP, back_rows(ks), LANES)
    return pl.pallas_call(
        functools.partial(fetch_kernel, ks, some),
        in_specs=[vmem] * (1 + len(some)) + ([] if into is None else [hbm_spec]),
        out_specs=hbm_spec,
        out_shape=pltpu.HBM(shape, BF),
        input_output_aliases={} if into is None else {1 + len(some): 0},
        scratch_shapes=[pltpu.VMEM(shape, BF), pltpu.SemaphoreType.DMA((shape[1] // CAP,))],
        compiler_params=params(12),
        name="fetch",
    )(ids, *[tables[k] for k in some], *(() if into is None else (into,)))


def unpack_kernel(ks, z_ref, g_ref, *refs):
    o_ref, block_ref, sems = refs[-3:]
    n = len(ks)
    copies = []

    def last_columns(slot, p, odd):
        for u in range(XC):
            get = lambda y: g_ref[u * NY + y, pl.ds((2 * n + p // 2) * CAP, CAP), :].astype(F32)
            for t in range(2):
                block_ref[slot, pl.ds(u * CAP, CAP), pl.ds(1024 + t * LANES, LANES)] = pair(
                    get(2 * t), get(2 * t + 1), odd
                ).astype(BF)

    def leave(slot, k, cols):
        piece = (slice(None), cols)
        copies.append(
            pltpu.make_async_copy(
                block_ref.at[slot].at[piece], o_ref.at[(z_ref[0] + k) % NZ].at[piece], sems.at[slot]
            )
        )
        copies[-1].start()

    for p, k in enumerate(ks):
        for u in range(XC):
            rows = pl.ds(u * CAP, CAP)
            for y in range(NY):
                block_ref[p, rows, pl.ds(y * LANES, LANES)] = g_ref[u * NY + y, pl.ds(p * CAP, CAP), :]
                block_ref[p, rows, pl.ds(512 + y * LANES, LANES)] = g_ref[u * NY + y, pl.ds((n + p) * CAP, CAP), :]
        if ks == FIRST and p == n - 1:
            leave(p, k, pl.ds(0, 1024))
        else:
            last_columns(p, p, p % 2 == 1)
            leave(p, k, pl.ds(0, 1280))
    if ks == LATER:
        last_columns(n, n - 1, True)
        leave(n, FIRST[-1], pl.ds(1024, 256))
    for copy in copies:
        copy.wait()


def unpack(z, ks, back, into=None):
    n = len(ks) + (ks == LATER)
    hbm_spec = pl.BlockSpec(memory_space=pltpu.HBM)
    return pl.pallas_call(
        functools.partial(unpack_kernel, ks),
        in_specs=[pl.BlockSpec(memory_space=pltpu.SMEM), pl.BlockSpec(memory_space=pltpu.VMEM)]
        + ([] if into is None else [hbm_spec]),
        out_specs=hbm_spec,
        out_shape=pltpu.HBM((NZ, XC * CAP, 1280), BF),
        input_output_aliases={} if into is None else {2: 0},
        scratch_shapes=[pltpu.VMEM((n, XC * CAP, 1280), BF), pltpu.SemaphoreType.DMA((n,))],
        compiler_params=params(8),
        cost_estimate=pl.CostEstimate(flops=0, bytes_accessed=700_000 * n, transcendentals=0),
        name="unpack",
    )(z, back, *(() if into is None else (into,)))


FULL_STEP = 48


def full_kernel(y_ref, *refs):
    g_refs, (w_ref, m_ref, v_ref, ow_ref, om_ref, ov_ref, all_ref) = refs[:NY], refs[NY:]
    for d in range(NY):
        all_ref[(y_ref[0] + d) % NY] = g_refs[d][...]
    for half in range(2):
        for t in range(10):
            if t < 8:
                grads = all_ref[t % NY, 2 * (t // NY) + half]
            else:
                grads = pair(all_ref[2 * (t - 8), 4], all_ref[2 * (t - 8) + 1, 4], half == 1)
            cols = pl.ds(t * LANES, LANES)
            w, m, v = adamw(w_ref[half, :, cols], m_ref[half, :, cols], v_ref[half, :, cols], grads)
            ow_ref[half, :, cols] = w
            om_ref[half, :, cols] = m
            ov_ref[half, :, cols] = v


def full_rows(y, grads, table_rows, first_moment, second_moment):
    wide = pl.BlockSpec((2, FULL_STEP, 1280), lambda i, s: (0, i, 0))
    part = pl.BlockSpec((5, FULL_STEP, LANES), lambda i, s: (0, i, 0))
    outs = pl.pallas_call(
        full_kernel,
        grid_spec=pltpu.PrefetchScalarGridSpec(
            num_scalar_prefetch=1,
            grid=(HALF // FULL_STEP,),
            in_specs=[part] * NY + [wide] * 3,
            out_specs=[wide] * 3,
            scratch_shapes=[pltpu.VMEM((NY, 5, FULL_STEP, LANES), F32)],
        ),
        out_shape=[pltpu.HBM((2, HALF, 1280), F32)] * 3,
        compiler_params=params(12),
        cost_estimate=pl.CostEstimate(flops=10_000_000, bytes_accessed=14_000_000, transcendentals=0),
        name="full_rows",
    )(
        y,
        *[g.reshape(5, HALF, LANES) for g in grads],
        *[hbm(t.reshape(2, HALF, 1280)) for t in (table_rows, first_moment, second_moment)],
    )
    return tuple(t.reshape(ROWS, 1280) for t in outs)


def along(value, axis, size, step):
    return lax.ppermute(value, axis, [(i, (i + step) % size) for i in range(size)])


def coded(x):
    root = jnp.sqrt(jnp.abs(x)) * 256.0
    return jnp.where(x < 0.0, -root, root).astype(F16)


def decoded(h):
    wide = h.astype(F32)
    return wide * jnp.abs(wide) * (1.0 / 65536.0)


def both_ways(up, down):
    up, down = lax.optimization_barrier((up, down))
    return lax.optimization_barrier((along(up, "z", NZ, 1), along(down, "z", NZ, -1)))


def send_sums(up, down):
    up, down = along(coded(up), "z", NZ, 1), along(coded(down), "z", NZ, -1)
    up, down = lax.optimization_barrier((up, down))
    return decoded(up), decoded(down)


def swap(x):
    return lax.all_to_all(x, SLAB, split_axis=0, concat_axis=0, tiled=True)


FAR, NEAR = (4, 3, 5), (2, 6, 1, 7, 0)
FIRST, LATER = (0, 1, 2, 6, 7), (3, 5, 4)


def local(table_rows, first_moment, second_moment, grad_rows, row_ids, next_ids):
    z = lax.axis_index("z").astype(jnp.int32)[None]
    y = lax.axis_index("y").astype(jnp.int32)[None]
    far = swap(pack_far(z, grad_rows, row_ids, next_ids))
    near = swap(pack(z, NEAR, grad_rows))
    mine = quarters(y, table_rows, first_moment, second_moment)
    part, (ids, wanted) = partial_sums(z, FAR, far)
    up = decoded(along(coded(part[4]), "z", NZ, 1))
    up, down = send_sums(part[3] + up, part[5])
    near, up, down = lax.optimization_barrier((near, up, down))
    part = partial_sums(z, NEAR, near, ids, (2, 6))
    up, down = send_sums(part[2] + up, part[6] + down)
    part = partial_sums(z, NEAR, near, ids, (1, 7, 0))
    up, down = send_sums(part[1] + up, part[7] + down)
    shared = coded(part[0] + up + down)
    summed = decoded(shared)
    own = adamw(*mine, summed)[0].astype(BF)
    grads = [shared] + [along(shared, "y", NY, -d) for d in range(1, NY)]
    tables = {0: own}
    tables[7], tables[1] = both_ways(own, own)
    found = fetch(FIRST, (0, 1, 7), wanted, tables)
    tables[6], tables[2], *grads[1:] = lax.optimization_barrier(
        (along(tables[7], "z", NZ, 1), along(tables[1], "z", NZ, -1), *grads[1:])
    )
    found = fetch(FIRST, (2, 6), wanted, tables, found)
    found, tables[6], tables[2] = lax.optimization_barrier((found, tables[6], tables[2]))
    back = swap(found)
    tables[5], tables[3] = both_ways(tables[6], tables[2])
    tables[4] = along(tables[5], "z", NZ, 1)
    back, found, *grads = lax.optimization_barrier((back, fetch(LATER, (7, *LATER), wanted, tables), *grads))
    backs = [back, swap(found)]
    outs = full_rows(y, [decoded(g) for g in grads], table_rows, first_moment, second_moment)
    fetched = unpack(z, LATER, backs[1], unpack(z, FIRST, backs[0]))
    return (*outs, fetched.reshape(NZ * XC * CAP, 1280))


def solution(mesh):
    fine = Mesh(mesh.devices.reshape(NY, NZ, 4, 2), ("y", "z", "x", "c"))
    owner = ("z", "x", "c")
    every = ("y", "z", "x", "c")
    return jax.shard_map(
        local,
        mesh=fine,
        in_specs=(P(owner, None), P(owner, None), P(owner, None), P(every, None), P(every), P(every)),
        out_specs=(P(owner, None), P(owner, None), P(owner, None), P(every, None)),
        check_vma=False,
    )
```

```python
import functools

import jax
import jax.numpy as jnp
from jax import lax
from jax.experimental import pallas as pl
from jax.experimental.pallas import tpu as pltpu
from jax.sharding import Mesh, PartitionSpec as P

STEP = 20
LANES = 128
CAP = 16
BF = jnp.bfloat16
F32 = jnp.float32
F16 = jnp.float16
SLAB = ("x", "c", "y")
GROUP = 32
NZ = 8
NY = 4
XC = 8
ROWS = 384
HALF = 192
QROWS = 960


def adamw(weights, first, second, grads):
    first_new = 0.9 * first + 0.1 * grads
    second_new = 0.95 * second + 0.05 * grads * grads
    corr_one = 1.0 - 0.9**STEP
    corr_two = 1.0 - 0.95**STEP
    update = first_new / corr_one / (jnp.sqrt(second_new / corr_two) + 1e-08) + 0.01 * weights
    return (weights - 0.1 * update, first_new, second_new)


def low_lanes(shape):
    return lax.broadcasted_iota(jnp.int32, shape, len(shape) - 1) < 64


def pair(a, b, upper):
    low = low_lanes(a.shape)
    axis = a.ndim - 1
    if isinstance(upper, bool):
        return jnp.where(low, pltpu.roll(a, 64, axis), b) if upper else jnp.where(low, a, pltpu.roll(b, 64, axis))
    return jnp.where(
        upper,
        jnp.where(low, pltpu.roll(a, 64, axis), b),
        jnp.where(low, a, pltpu.roll(b, 64, axis)),
    )


def centred(rows):
    return (rows.astype(F32) - HALF).astype(BF)


def one_hot(rows, ids):
    return jnp.where(rows == ids, jnp.ones((), BF), jnp.zeros((), BF))


def params(mib):
    return pltpu.CompilerParams(vmem_limit_bytes=mib * 1024 * 1024)


def hbm(x):
    return pltpu.with_memory_space_constraint(x, pltpu.HBM)


def tile_iota(axis):
    return lax.broadcasted_iota(jnp.int32, (8, LANES), axis)


def diagonal(rolled, shift):
    moved = pltpu.roll(rolled, (NZ * LANES - CAP * shift) % LANES, 1)
    kept = jnp.where(tile_iota(1) // CAP == tile_iota(0), moved, 0.0)
    return jnp.sum(kept, axis=0, keepdims=True)


def row_roll(x):
    return pltpu.roll(x, 0, 1, stride=CAP, stride_axis=0)


def chunk_rows(n):
    return 2 * CAP * n + CAP * ((n + 1) // 2)


def pack_kernel(n, step, with_ids, z_ref, *refs):
    blocks, o_ref = refs[:n], refs[-1]
    sub = lax.broadcasted_iota(jnp.int32, (CAP, LANES), 0)
    if with_ids:
        ids = [row_roll(r[...].astype(F32)) for r in refs[n : n + 2]]
    for u in range(step):
        rest = jnp.zeros((CAP, LANES), F32)
        if with_ids:
            for t in range(2):
                mine = diagonal(ids[t], pl.program_id(0) * step + u)
                upper = jnp.floor(mine * (1.0 / 16.0))
                lower = mine - 16.0 * upper
                for r, row in enumerate((pltpu.roll(upper, 64, 1), upper, pltpu.roll(lower, 64, 1), lower)):
                    rest = jnp.where(sub == 4 * t + r, row, rest)
        for y in range(NY):
            for p in range(n):
                o_ref[u, y, pl.ds(p * CAP, CAP), :] = blocks[p][0, u, :, pl.ds(y * LANES, LANES)]
                o_ref[u, y, pl.ds((n + p) * CAP, CAP), :] = blocks[p][0, u, :, pl.ds(512 + y * LANES, LANES)]
            cols = pl.ds(1024 + (y // 2) * LANES, LANES)
            for t in range((n + 1) // 2):
                a = blocks[2 * t][0, u, :, cols].astype(F32)
                if 2 * t + 1 < n:
                    tile = pair(a, blocks[2 * t + 1][0, u, :, cols].astype(F32), y % 2 == 1)
                else:
                    tile = jnp.where(low_lanes(a.shape), pltpu.roll(a, 64, 1) if y % 2 else a, rest)
                o_ref[u, y, pl.ds((2 * n + t) * CAP, CAP), :] = tile.astype(BF)


def pack(z, ks, grad_rows, ids=()):
    n, step = len(ks), 4
    rows = chunk_rows(n)
    whole = pl.BlockSpec((8, LANES), lambda i, s: (0, 0))
    block = lambda k: pl.BlockSpec((1, step, CAP, 1280), lambda i, s: ((s[0] + k) % NZ, i, 0, 0))
    grads = hbm(grad_rows.reshape(NZ, XC, CAP, 1280))
    out = pl.pallas_call(
        functools.partial(pack_kernel, n, step, bool(ids)),
        grid_spec=pltpu.PrefetchScalarGridSpec(
            num_scalar_prefetch=1,
            grid=(XC // step,),
            in_specs=[block(k) for k in ks] + [whole for _ in ids],
            out_specs=pl.BlockSpec((step, NY, rows, LANES), lambda i, s: (i, 0, 0, 0)),
        ),
        out_shape=pltpu.HBM((XC, NY, rows, LANES), BF),
        compiler_params=params(14),
        cost_estimate=pl.CostEstimate(flops=0, bytes_accessed=700_000 * n, transcendentals=0),
        name="pack",
    )(z, *[grads] * n, *[hbm(i.reshape(8, LANES)) for i in ids])
    return out.reshape(GROUP, rows, LANES)


def read_ids(z_ref, got_ref, at, outs):
    sub = tile_iota(0)
    low = low_lanes((8, LANES))
    for q in range(GROUP // 8):
        tiles = [jnp.zeros((8, LANES), F32)] * 4
        for j in range(8):
            head = got_ref[8 * q + j, pl.ds(at, CAP), :].astype(F32)
            for t in range(4):
                row = 4 * (t // 2) + t % 2
                mine = head[row : row + 1] * 16.0 + head[row + 2 : row + 3]
                tiles[t] = jnp.where(sub == j, mine, tiles[t])
        for t, ref in enumerate(outs):
            rolled = row_roll(jnp.where(low, pltpu.roll(tiles[2 * t], 64, 1), tiles[2 * t + 1]))
            for k in range(NZ):
                ref[pl.ds(k, 1), pl.ds(q * LANES, LANES)] = diagonal(rolled, z_ref[0] + k).astype(jnp.int32)


def sums_kernel(ks, first, wanted, z_ref, *refs):
    n = len(ks)
    if first:
        got_ref, outs, ids_ref = refs[0], refs[1 : 1 + n], refs[1 + n]
        read_ids(z_ref, got_ref, (2 * n + n // 2) * CAP, refs[1 + n :])
    else:
        got_ref, ids_ref, outs = refs[0], refs[1], refs[2:]
    rows = centred(lax.broadcasted_iota(jnp.int32, (ROWS, GROUP * CAP), 0))
    for out_ref, k in zip(outs, wanted):
        p = ks.index(k)
        pick = one_hot(rows, centred(ids_ref[pl.ds(k, 1), :]))
        slots = jnp.concatenate(
            [
                got_ref[:, pl.ds(at * CAP, CAP), :].reshape(GROUP * CAP, LANES)
                for at in (p, n + p, 2 * n + p // 2)
            ],
            axis=1,
        )
        total = jnp.dot(pick, slots, preferred_element_type=F32)
        out_ref[pl.ds(0, ROWS), :] = total[:, :128]
        out_ref[pl.ds(ROWS, ROWS), :] = total[:, 128:256]
        last = total[:, 256:]
        out_ref[pl.ds(2 * ROWS, HALF), :] = pair(last[:HALF], last[HALF:], p % 2 == 1)


def partial_sums(z, ks, got, ids=None, wanted=None):
    vmem = pl.BlockSpec(memory_space=pltpu.VMEM)
    first = ids is None
    wanted = wanted or ks
    ids_shape = jax.ShapeDtypeStruct((NZ, GROUP * CAP), jnp.int32)
    outs = [jax.ShapeDtypeStruct((QROWS, LANES), F32)] * len(wanted) + [ids_shape] * (2 if first else 0)
    got = pl.pallas_call(
        functools.partial(sums_kernel, ks, first, wanted),
        in_specs=[pl.BlockSpec(memory_space=pltpu.SMEM)] + [vmem] * (1 if first else 2),
        out_specs=[vmem] * len(outs),
        out_shape=outs,
        compiler_params=params(12),
        name="partial_sums",
    )(z, got, *(() if first else (ids,)))
    sums = dict(zip(wanted, got))
    return (sums, tuple(got[len(ks) :])) if first else sums


def quarter_kernel(y_ref, *refs):
    odd = y_ref[0] % 2 == 1
    for i in range(3):
        a, b, c = (r[...] for r in refs[3 * i : 3 * i + 3])
        o_ref = refs[9 + i]
        o_ref[pl.ds(0, ROWS), :] = a
        o_ref[pl.ds(ROWS, ROWS), :] = b
        o_ref[pl.ds(2 * ROWS, HALF), :] = pair(c[:HALF], c[HALF:], odd)


def quarters(y, *arrays):
    spec = [
        pl.BlockSpec((ROWS, LANES), lambda i, s: (0, s[0])),
        pl.BlockSpec((ROWS, LANES), lambda i, s: (0, NY + s[0])),
        pl.BlockSpec((ROWS, LANES), lambda i, s: (0, 2 * NY + s[0] // 2)),
    ]
    return pl.pallas_call(
        quarter_kernel,
        grid_spec=pltpu.PrefetchScalarGridSpec(
            num_scalar_prefetch=1,
            grid=(1,),
            in_specs=spec * 3,
            out_specs=[pl.BlockSpec((QROWS, LANES), lambda i, s: (0, 0))] * 3,
        ),
        out_shape=[jax.ShapeDtypeStruct((QROWS, LANES), F32)] * 3,
        compiler_params=params(12),
        cost_estimate=pl.CostEstimate(flops=1_000_000, bytes_accessed=3_000_000, transcendentals=0),
        name="quarters",
    )(y, *[hbm(t) for t in arrays for _ in range(3)])


def back_rows(ks):
    return chunk_rows(len(ks)) - (CAP if ks == FIRST else 0)


def fetch_kernel(ks, some, ids_ref, *refs):
    n = len(ks)
    tables, (out_ref, o_ref, sems) = refs[: len(some)], refs[-3:]
    rows = centred(lax.broadcasted_iota(jnp.int32, (GROUP * CAP, ROWS), 1))
    columns = jnp.transpose(ids_ref[...].astype(F32) - HALF).astype(BF)
    low = low_lanes((GROUP, CAP, LANES))
    even = rest = None
    copies = []

    def leave(at, value):
        piece = (slice(None), pl.ds(at * CAP, CAP))
        o_ref[piece] = value
        copies.append(pltpu.make_async_copy(o_ref.at[piece], out_ref.at[piece], sems.at[at]))
        copies[-1].start()

    def find(k, wide):
        found = jnp.dot(one_hot(rows, columns[:, k : k + 1]), wide, preferred_element_type=F32)
        return found.astype(BF).reshape(GROUP, CAP, wide.shape[1])

    for table, k in zip(tables, some):
        p = ks.index(k) if k in ks else -1
        last = table[pl.ds(2 * ROWS, HALF), :]
        moved = pltpu.roll(last.astype(F32), 64, 1).astype(BF)
        ends = jnp.concatenate([moved, last] if p % 2 else [last, moved], axis=0)
        if p < 0:
            rest = find(k, ends)
            continue
        found = find(k, jnp.concatenate([table[pl.ds(0, ROWS), :], table[pl.ds(ROWS, ROWS), :], ends], axis=1))
        leave(p, found[:, :, :128])
        leave(n + p, found[:, :, 128:256])
        if p % 2:
            leave(2 * n + p // 2, jnp.where(low, even, found[:, :, 256:]))
        elif p < n - 1:
            even = found[:, :, 256:]
        elif rest is not None:
            leave(2 * n + p // 2, jnp.where(low, found[:, :, 256:], rest))
    for copy in copies:
        copy.wait()


def fetch(ks, some, ids, tables, into=None):
    vmem = pl.BlockSpec(memory_space=pltpu.VMEM)
    hbm_spec = pl.BlockSpec(memory_space=pltpu.HBM)
    shape = (GROUP, back_rows(ks), LANES)
    return pl.pallas_call(
        functools.partial(fetch_kernel, ks, some),
        in_specs=[vmem] * (1 + len(some)) + ([] if into is None else [hbm_spec]),
        out_specs=hbm_spec,
        out_shape=pltpu.HBM(shape, BF),
        input_output_aliases={} if into is None else {1 + len(some): 0},
        scratch_shapes=[pltpu.VMEM(shape, BF), pltpu.SemaphoreType.DMA((shape[1] // CAP,))],
        compiler_params=params(12),
        name="fetch",
    )(ids, *[tables[k] for k in some], *(() if into is None else (into,)))


def unpack_kernel(ks, z_ref, g_ref, *refs):
    o_ref, block_ref, sems = refs[-3:]
    n = len(ks)
    copies = []

    def last_columns(slot, p, odd):
        for u in range(XC):
            get = lambda y: g_ref[u * NY + y, pl.ds((2 * n + p // 2) * CAP, CAP), :].astype(F32)
            for t in range(2):
                block_ref[slot, pl.ds(u * CAP, CAP), pl.ds(1024 + t * LANES, LANES)] = pair(
                    get(2 * t), get(2 * t + 1), odd
                ).astype(BF)

    def leave(slot, k, cols):
        piece = (slice(None), cols)
        copies.append(
            pltpu.make_async_copy(
                block_ref.at[slot].at[piece], o_ref.at[(z_ref[0] + k) % NZ].at[piece], sems.at[slot]
            )
        )
        copies[-1].start()

    for p, k in enumerate(ks):
        for u in range(XC):
            rows = pl.ds(u * CAP, CAP)
            for y in range(NY):
                block_ref[p, rows, pl.ds(y * LANES, LANES)] = g_ref[u * NY + y, pl.ds(p * CAP, CAP), :]
                block_ref[p, rows, pl.ds(512 + y * LANES, LANES)] = g_ref[u * NY + y, pl.ds((n + p) * CAP, CAP), :]
        if ks == FIRST and p == n - 1:
            leave(p, k, pl.ds(0, 1024))
        else:
            last_columns(p, p, p % 2 == 1)
            leave(p, k, pl.ds(0, 1280))
    if ks == LATER:
        last_columns(n, n - 1, True)
        leave(n, FIRST[-1], pl.ds(1024, 256))
    for copy in copies:
        copy.wait()


def unpack(z, ks, back, into=None):
    n = len(ks) + (ks == LATER)
    hbm_spec = pl.BlockSpec(memory_space=pltpu.HBM)
    return pl.pallas_call(
        functools.partial(unpack_kernel, ks),
        in_specs=[pl.BlockSpec(memory_space=pltpu.SMEM), pl.BlockSpec(memory_space=pltpu.VMEM)]
        + ([] if into is None else [hbm_spec]),
        out_specs=hbm_spec,
        out_shape=pltpu.HBM((NZ, XC * CAP, 1280), BF),
        input_output_aliases={} if into is None else {2: 0},
        scratch_shapes=[pltpu.VMEM((n, XC * CAP, 1280), BF), pltpu.SemaphoreType.DMA((n,))],
        compiler_params=params(8),
        cost_estimate=pl.CostEstimate(flops=0, bytes_accessed=700_000 * n, transcendentals=0),
        name="unpack",
    )(z, back, *(() if into is None else (into,)))


FULL_STEP = 48


def full_kernel(y_ref, *refs):
    g_refs, (w_ref, m_ref, v_ref, ow_ref, om_ref, ov_ref, all_ref) = refs[:NY], refs[NY:]
    for d in range(NY):
        all_ref[(y_ref[0] + d) % NY] = g_refs[d][...]
    for half in range(2):
        for t in range(10):
            if t < 8:
                grads = all_ref[t % NY, 2 * (t // NY) + half]
            else:
                grads = pair(all_ref[2 * (t - 8), 4], all_ref[2 * (t - 8) + 1, 4], half == 1)
            cols = pl.ds(t * LANES, LANES)
            w, m, v = adamw(w_ref[half, :, cols], m_ref[half, :, cols], v_ref[half, :, cols], grads)
            ow_ref[half, :, cols] = w
            om_ref[half, :, cols] = m
            ov_ref[half, :, cols] = v


def full_rows(y, grads, table_rows, first_moment, second_moment):
    wide = pl.BlockSpec((2, FULL_STEP, 1280), lambda i, s: (0, i, 0))
    part = pl.BlockSpec((5, FULL_STEP, LANES), lambda i, s: (0, i, 0))
    outs = pl.pallas_call(
        full_kernel,
        grid_spec=pltpu.PrefetchScalarGridSpec(
            num_scalar_prefetch=1,
            grid=(HALF // FULL_STEP,),
            in_specs=[part] * NY + [wide] * 3,
            out_specs=[wide] * 3,
            scratch_shapes=[pltpu.VMEM((NY, 5, FULL_STEP, LANES), F32)],
        ),
        out_shape=[pltpu.HBM((2, HALF, 1280), F32)] * 3,
        compiler_params=params(12),
        cost_estimate=pl.CostEstimate(flops=10_000_000, bytes_accessed=14_000_000, transcendentals=0),
        name="full_rows",
    )(
        y,
        *[g.reshape(5, HALF, LANES) for g in grads],
        *[hbm(t.reshape(2, HALF, 1280)) for t in (table_rows, first_moment, second_moment)],
    )
    return tuple(t.reshape(ROWS, 1280) for t in outs)


def along(value, axis, size, step):
    return lax.ppermute(value, axis, [(i, (i + step) % size) for i in range(size)])


def coded(x):
    root = jnp.sqrt(jnp.abs(x)) * 256.0
    return jnp.where(x < 0.0, -root, root).astype(F16)


def decoded(h):
    wide = h.astype(F32)
    return wide * jnp.abs(wide) * (1.0 / 65536.0)


def both_ways(up, down):
    up, down = lax.optimization_barrier((up, down))
    return lax.optimization_barrier((along(up, "z", NZ, 1), along(down, "z", NZ, -1)))


def send_sums(up, down):
    up, down = along(coded(up), "z", NZ, 1), along(coded(down), "z", NZ, -1)
    up, down = lax.optimization_barrier((up, down))
    return decoded(up), decoded(down)


def swap(x):
    return lax.all_to_all(x, SLAB, split_axis=0, concat_axis=0, tiled=True)


FAR, NEAR = (4, 3, 5), (2, 6, 1, 7, 0)
FIRST, LATER = (0, 1, 2, 6, 7), (3, 5, 4)


def local(table_rows, first_moment, second_moment, grad_rows, row_ids, next_ids):
    z = lax.axis_index("z").astype(jnp.int32)[None]
    y = lax.axis_index("y").astype(jnp.int32)[None]
    far = swap(pack(z, FAR, grad_rows, (row_ids, next_ids)))
    near = swap(pack(z, NEAR, grad_rows))
    mine = quarters(y, table_rows, first_moment, second_moment)
    part, (ids, wanted) = partial_sums(z, FAR, far)
    up = decoded(along(coded(part[4]), "z", NZ, 1))
    up, down = send_sums(part[3] + up, part[5])
    near, up, down = lax.optimization_barrier((near, up, down))
    part = partial_sums(z, NEAR, near, ids, (2, 6))
    up, down = send_sums(part[2] + up, part[6] + down)
    part = partial_sums(z, NEAR, near, ids, (1, 7, 0))
    up, down = send_sums(part[1] + up, part[7] + down)
    shared = coded(part[0] + up + down)
    summed = decoded(shared)
    own = adamw(*mine, summed)[0].astype(BF)
    grads = [shared] + [along(shared, "y", NY, -d) for d in range(1, NY)]
    tables = {0: own}
    tables[7], tables[1] = along(own, "z", NZ, 1), along(own, "z", NZ, -1)
    found = fetch(FIRST, (0, 1, 7), wanted, tables)
    tables[6], tables[2], *grads[1:] = lax.optimization_barrier(
        (along(tables[7], "z", NZ, 1), along(tables[1], "z", NZ, -1), *grads[1:])
    )
    found = fetch(FIRST, (2, 6), wanted, tables, found)
    found, tables[6], tables[2] = lax.optimization_barrier((found, tables[6], tables[2]))
    back = swap(found)
    tables[5], tables[3] = both_ways(tables[6], tables[2])
    tables[4] = along(tables[5], "z", NZ, 1)
    back, found, *grads = lax.optimization_barrier((back, fetch(LATER, (7, *LATER), wanted, tables), *grads))
    backs = [back, swap(found)]
    outs = full_rows(y, [decoded(g) for g in grads], table_rows, first_moment, second_moment)
    fetched = unpack(z, LATER, backs[1], unpack(z, FIRST, backs[0]))
    return (*outs, fetched.reshape(NZ * XC * CAP, 1280))


def solution(mesh):
    fine = Mesh(mesh.devices.reshape(NY, NZ, 4, 2), ("y", "z", "x", "c"))
    owner = ("z", "x", "c")
    every = ("y", "z", "x", "c")
    return jax.shard_map(
        local,
        mesh=fine,
        in_specs=(P(owner, None), P(owner, None), P(owner, None), P(every, None), P(every), P(every)),
        out_specs=(P(owner, None), P(owner, None), P(owner, None), P(every, None)),
        check_vma=False,
    )
```
